32 devices in a mesh: groups: 2 (over y), tm: 4 (over z), mp: 2 (over x), sub: 2 (over core).
Axes of the slice: x: 2, y: 2, z: 4, core: 2. Of those that a mesh axis runs over, the one named last changes fastest.
Arguments:
- events: bfloat16 [16384, 768], P(('groups', 'tm', 'sub')), parts along dimension 0, may hold values from -6 to 6
- w_gate: bfloat16 [768, 1536], P(None, 'mp'), may hold values from -0.21875 to 0.21875
- w_inner: bfloat16 [768, 1536], P(None, 'mp'), may hold values from -0.21875 to 0.21875
- w_bc: bfloat16 [768, 256], replicated, may hold values from -0.21875 to 0.21875
- w_step: bfloat16 [768, 24], P(None, 'mp'), may hold values from -0.21875 to 0.21875
- step_bias: float32 [24], P('mp'), may hold values from -3 to 1
- log_decay: float32 [24, 16384], P('mp', ('groups', 'tm', 'sub')), parts along dimension 1, may hold values from -1 to 0
- norm_gain: float32 [1536], P('mp'), may hold values from 0.1 to 1.9
- w_out: bfloat16 [1536, 768], P('mp'), may hold values from -0.15625 to 0.15625
- mix_gain: float32 [768], replicated, may hold values from 0.1 to 1.9
- port: int32 [16384], P(('groups', 'tm', 'sub')), parts along dimension 0, may hold values from 0 to 15, as said below
- port_shard: int32 [32], P('groups'), parts along dimension 0, may hold values from 0 to 3, as said below
- w_up: bfloat16 [4, 768, 1536], P('tm', None, 'mp'), may hold values from -0.21875 to 0.21875
- b_up: float32 [4, 1536], P('tm', 'mp'), may hold values from -6 to 6
- w_down: bfloat16 [4, 1536, 768], P('tm', 'mp'), may hold values from -0.15625 to 0.15625
Outputs:
- readout: bfloat16 [16384, 768], P(('groups', 'tm', 'sub'), 'mp'), parts along dimension 0
The draws below stay inside these ranges and needn't reach their ends.
There are 2 independent parts, one for each index of `groups`. The reference program is written for one: setup_inputs(seed, part) draws one part's arguments, and reference() takes and returns one part's arrays. A program takes and returns all parts, laid end to end along the dimension named above; an argument that names none is the same for every part. Nothing has to cross between parts.
Inputs may be any that keep to these rules, and one draw needn't show every extreme that they name: Of the 1024 events of one device (aligned blocks of the trace, in order over tm and sub), exactly 512 belong to one port group, the same group for all devices of a trace and drawn per trace, and the rest are spread as evenly as possible over the other groups, so no device has more than 512 events of one group. Within a group, some ports are more frequent than others. `port_shard`: each port group owns exactly 4 ports.
All inputs are finite; a program needn't handle non-finite values.
Results may differ from the reference program's by a relative error of at most 0.02.
Values may be sent and summed in bfloat16 or wider, within the bound.
No kernel may reach another device: no remote copies, remote signals or barrier semaphores. Data moves between devices by JAX's collectives and lax.ppermute only.
A program may use at most 64 MiB of HBM per device.

```python
import jax
import jax.numpy as jnp
from jax import lax

MODEL_WIDTH = 768
ATTENTION_LANES = 24
HEAD_DIM = 64
INNER = 1536
NSTATE = 128
READOUT_UNITS = 1536
BLOCK = 256
PORTS_SHARD = 4
TOK_DEV = 1024
LOGGED_ARRIVALS = 8192
CAP = 512
PORTS = 16
PORT_GROUPS = 4
N_TM = 4
N_MP = 2
N_SUB = 2


spike_total = 3


def port_ranking(key):
    return jax.random.permutation(jax.random.fold_in(key, 7), PORTS)


def draw_port_shard(key, part):
    return (port_ranking(key) % N_TM).astype(jnp.int32)


def draw_port(key, part):
    ranking_table = port_ranking(key)
    port_owner = jnp.argsort(ranking_table)
    blocks = LOGGED_ARRIVALS // TOK_DEV
    hottest = jax.random.randint(jax.random.fold_in(key, 8), (), 0, N_TM)
    random_seed_stream = jax.random.split(jax.random.fold_in(key, 9), blocks)
    ranking = jax.vmap(lambda block_key: jax.random.permutation(block_key, TOK_DEV))(random_seed_stream)
    offsets = jax.random.randint(jax.random.fold_in(key, 10), (blocks, 1), 0, N_TM - 1)
    others = (hottest + 1 + (ranking - CAP + offsets) % (N_TM - 1)) % N_TM
    dest_shard = jnp.where(ranking < CAP, hottest, others)
    first_draw = jax.random.randint(jax.random.fold_in(key, 11), (blocks, TOK_DEV), 0, PORTS_SHARD)
    second_draw = jax.random.randint(jax.random.fold_in(key, 12), (blocks, TOK_DEV), 0, PORTS_SHARD)
    pick_rank = jnp.minimum(first_draw, second_draw)
    return port_owner[dest_shard + N_TM * pick_rank].reshape(LOGGED_ARRIVALS).astype(jnp.int32)


def draw_log_decay(key, part):
    random_seed_stream = [jax.random.fold_in(key, 20 + number) for number in range(8)]
    fast_share = 0.5
    fast_head = jax.random.uniform(random_seed_stream[0], (ATTENTION_LANES, 1)) < fast_share
    fast_rate = jnp.exp(jax.random.uniform(random_seed_stream[1], (ATTENTION_LANES, 1), minval=jnp.log(1.0 / 50.0), maxval=jnp.log(1.0 / 30.0)))
    slow_rate = jnp.exp(jax.random.uniform(random_seed_stream[2], (ATTENTION_LANES, 1), minval=jnp.log(0.05), maxval=jnp.log(0.3))) / LOGGED_ARRIVALS
    fading_speed = jnp.where(fast_head, fast_rate, slow_rate)
    segment_multiplier = jnp.exp(jax.random.uniform(random_seed_stream[3], (ATTENTION_LANES, LOGGED_ARRIVALS // BLOCK, 1), minval=-0.5, maxval=0.5))
    segment_multiplier = jnp.broadcast_to(segment_multiplier, (ATTENTION_LANES, LOGGED_ARRIVALS // BLOCK, BLOCK)).reshape(ATTENTION_LANES, LOGGED_ARRIVALS)
    arrival_jitter = jax.random.uniform(random_seed_stream[4], (ATTENTION_LANES, LOGGED_ARRIVALS), minval=0.5, maxval=1.5)
    arrival_positions = jax.random.randint(random_seed_stream[5], (spike_total,), 0, LOGGED_ARRIVALS)
    spike_arrivals = jnp.any(jnp.arange(LOGGED_ARRIVALS)[None, :] == arrival_positions[:, None], axis=0)
    spike_length = jnp.log(jax.random.uniform(random_seed_stream[6], (ATTENTION_LANES, LOGGED_ARRIVALS), minval=0.55, maxval=0.8))
    payload_entries = -fading_speed * segment_multiplier * arrival_jitter + jnp.where(spike_arrivals[None, :], spike_length, 0.0)
    return payload_entries.astype(jnp.float32)


def steps_of(stream_key, dims, cuts, least, largest):
    def one(dim, shards_of):
        heights = jax.random.uniform(jax.random.fold_in(jax.random.fold_in(stream_key, 6), dim), (shards_of,), jnp.float32, least / len(cuts), largest / len(cuts))
        return jnp.repeat(jnp.exp(heights), dims[dim] // shards_of).reshape((-1,) + (1,) * (len(dims) - dim - 1))

    level = one(*cuts[0])
    for cut in cuts[1:]:
        level = level * one(*cut)
    return level


def centred(stream_key, extent, scale, bound, pieces=(), held_as=jnp.bfloat16):
    values = scale * jax.random.normal(stream_key, extent, jnp.float32)
    if pieces:
        values = values * steps_of(stream_key, extent, pieces, -0.22, 0.18)
    return jnp.clip(values, -bound, bound).astype(held_as)


def setup_inputs(seed: int = 0, part: int = 0) -> dict:
    keys = jax.random.split(jax.random.key(seed), 16)
    part_keys = jax.random.split(jax.random.fold_in(keys[15], part), 16)
    return {
        "events": centred(part_keys[0], (LOGGED_ARRIVALS, MODEL_WIDTH), 1.0, 6.0, ((0, 8),)),
        "w_gate": centred(keys[1], (MODEL_WIDTH, INNER), MODEL_WIDTH ** -0.5, 0.21875, ((1, 2),)),
        "w_inner": centred(keys[2], (MODEL_WIDTH, INNER), MODEL_WIDTH ** -0.5, 0.21875, ((1, 2),)),
        "w_bc": centred(keys[3], (MODEL_WIDTH, 2 * NSTATE), MODEL_WIDTH ** -0.5, 0.21875),
        "w_step": centred(keys[4], (MODEL_WIDTH, ATTENTION_LANES), MODEL_WIDTH ** -0.5, 0.21875, ((1, 2),)),
        "step_bias": jnp.clip(-3.0 + 4.0 * jax.random.uniform(keys[5], (ATTENTION_LANES,), jnp.float32) ** steps_of(keys[5], (ATTENTION_LANES,), ((0, 2),), -0.2, 0.2), -3.0, 1.0),
        "log_decay": draw_log_decay(jax.random.fold_in(jax.random.fold_in(keys[15], part), 71), part),
        "norm_gain": jnp.clip(1.0 + 0.18 * jax.random.normal(keys[7], (INNER,), jnp.float32), 0.1, 1.9),
        "w_out": centred(keys[8], (INNER, MODEL_WIDTH), INNER ** -0.5, 0.15625, ((0, 2),)),
        "mix_gain": jnp.clip(1.0 + 0.18 * jax.random.normal(keys[9], (MODEL_WIDTH,), jnp.float32), 0.1, 1.9),
        "port": draw_port(jax.random.fold_in(jax.random.fold_in(keys[15], part), 71), part),
        "port_shard": draw_port_shard(jax.random.fold_in(jax.random.fold_in(keys[15], part), 71), part),
        "w_up": centred(keys[12], (PORT_GROUPS, MODEL_WIDTH, READOUT_UNITS), MODEL_WIDTH ** -0.5, 0.21875, ((0, 4), (2, 2))),
        "b_up": centred(keys[13], (PORT_GROUPS, READOUT_UNITS), 1.0, 6.0, ((0, 4), (1, 2)), jnp.float32),
        "w_down": centred(keys[14], (PORT_GROUPS, READOUT_UNITS, MODEL_WIDTH), READOUT_UNITS ** -0.5, 0.15625, ((0, 4), (1, 2))),
    }


def scan_block(state, inputs):
    b_part, c_part, x_part, decay_part = inputs
    running = jnp.cumsum(decay_part, axis=1)
    causal_mask = jnp.arange(BLOCK)[:, None] >= jnp.arange(BLOCK)[None, :]
    spread = running[:, :, None] - running[:, None, :]
    weights = jnp.where(causal_mask[None], jnp.exp(jnp.where(causal_mask[None], spread, 0.0)), 0.0)
    affinity = jnp.dot(c_part, b_part.T, preferred_element_type=jnp.float32)
    x_float = x_part.astype(jnp.float32)
    within = jnp.einsum('hij,jhp->ihp', affinity[None] * weights, x_float, precision=lax.Precision.HIGHEST)
    c_float = c_part.astype(jnp.float32)
    carried = jnp.einsum('in,hi,hnp->ihp', c_float, jnp.exp(running), state, precision=lax.Precision.HIGHEST)
    to_end = jnp.exp(running[:, -1:] - running)
    fresh = jnp.einsum('jn,hj,jhp->hnp', b_part.astype(jnp.float32), to_end, x_float, precision=lax.Precision.HIGHEST)
    new_state = jnp.exp(running[:, -1])[:, None, None] * state + fresh
    return (new_state, within + carried)

def reference(events, w_gate, w_inner, w_bc, w_step, step_bias, log_decay, norm_gain, w_out, mix_gain, port, port_shard, w_up, b_up, w_down):
    gate_pre = jnp.dot(events, w_gate, preferred_element_type=jnp.float32)
    inner_pre = jnp.dot(events, w_inner, preferred_element_type=jnp.float32)
    bc_proj = jnp.dot(events, w_bc, preferred_element_type=jnp.float32).astype(jnp.bfloat16)
    step_size = jax.nn.softplus(jnp.dot(events, w_step, preferred_element_type=jnp.float32) + step_bias[None, :])
    scaled = (inner_pre.reshape(LOGGED_ARRIVALS, ATTENTION_LANES, HEAD_DIM) * step_size[:, :, None]).astype(jnp.bfloat16)
    blocks = LOGGED_ARRIVALS // BLOCK
    b_blocks = bc_proj[:, :NSTATE].reshape(blocks, BLOCK, NSTATE)
    c_blocks = bc_proj[:, NSTATE:].reshape(blocks, BLOCK, NSTATE)
    x_blocks = scaled.reshape(blocks, BLOCK, ATTENTION_LANES, HEAD_DIM)
    decay_blocks = log_decay.reshape(ATTENTION_LANES, blocks, BLOCK).transpose(1, 0, 2)
    start = jnp.zeros((ATTENTION_LANES, NSTATE, HEAD_DIM), jnp.float32)
    final_state, outputs = lax.scan(scan_block, start, (b_blocks, c_blocks, x_blocks, decay_blocks))
    ssm_out = outputs.reshape(LOGGED_ARRIVALS, ATTENTION_LANES, HEAD_DIM)
    gated = ssm_out * jax.nn.silu(gate_pre.reshape(LOGGED_ARRIVALS, ATTENTION_LANES, HEAD_DIM))
    square_mean = lax.optimization_barrier(jnp.mean(gated * gated, axis=2, keepdims=True))
    normed = (gated * lax.rsqrt(square_mean + 1e-05) * norm_gain.reshape(ATTENTION_LANES, HEAD_DIM)).reshape(LOGGED_ARRIVALS, INNER).astype(jnp.bfloat16)
    layer_out = jnp.dot(normed, w_out, preferred_element_type=jnp.float32)
    feature_mean = lax.optimization_barrier(jnp.mean(layer_out * layer_out, axis=1, keepdims=True))
    ready = (layer_out * lax.rsqrt(feature_mean + 1e-05) * mix_gain[None, :]).astype(jnp.bfloat16)
    target = port_shard[port]
    queue_buffer_size = N_SUB * N_TM * CAP

    def group_step(result, inputs):
        group_id, up_weight, up_bias, down_matrix = inputs
        member = target == group_id
        position = (jnp.cumsum(member.astype(jnp.int32)) - 1).astype(jnp.int32)
        placed = jnp.where(member, position, queue_buffer_size).astype(jnp.int32)
        gathered = jnp.zeros((queue_buffer_size, MODEL_WIDTH), jnp.bfloat16).at[placed].set(ready, mode='drop')
        hidden_units = jax.nn.gelu(jnp.dot(gathered, up_weight, preferred_element_type=jnp.float32) + up_bias[None, :], approximate=True).astype(jnp.bfloat16)
        trace_pieces = jnp.einsum('ojg,jgq->ojq', hidden_units.reshape(queue_buffer_size, N_MP, READOUT_UNITS // N_MP).astype(jnp.float32), down_matrix.reshape(N_MP, READOUT_UNITS // N_MP, MODEL_WIDTH).astype(jnp.float32))
        rounded = lax.optimization_barrier(trace_pieces.astype(jnp.bfloat16))
        summed = lax.optimization_barrier(jnp.sum(rounded.astype(jnp.float32), axis=1)).astype(jnp.bfloat16)
        picked = summed[jnp.clip(position, 0, queue_buffer_size - 1)]
        return (jnp.where(member[:, None], picked, result), None)
    readout, unused = lax.scan(group_step, jnp.zeros((LOGGED_ARRIVALS, MODEL_WIDTH), jnp.bfloat16), (jnp.arange(PORT_GROUPS, dtype=jnp.int32), w_up, b_up, w_down))
    return readout
```

```python
import jax
import jax.numpy as jnp
from jax import lax
from jax.experimental import pallas as pl
from jax.experimental.pallas import tpu as pltpu
from jax.sharding import PartitionSpec as P

BLOCK = 256
F32 = jnp.float32
BF16 = jnp.bfloat16


def entering_2(shard, axis, join, neutral):
    place = lax.axis_index(axis)
    gathered = jax.tree.map(
        lambda a, kind: lax.all_gather(a.astype(kind), axis),
        shard,
        jax.tree.map(lambda a: jnp.bfloat16 if a.dtype == jnp.float32 else a.dtype, shard),
    )
    state = jax.tree.map(lambda a, e: jnp.zeros_like(a) + jnp.asarray(e, a.dtype), shard, neutral)

    def one(hop, state):
        return join(
            state,
            jax.tree.map(
                lambda a, own: lax.dynamic_index_in_dim(a, hop, 0, False).astype(own.dtype),
                gathered,
                shard,
            ),
        )

    return lax.fori_loop(0, place, one, state)


def combine_states(earlier, later):
    decay_early, state_early = earlier
    decay_late, state_late = later
    return (decay_early * decay_late, decay_late[:, None, None] * state_early + state_late)


def place_rows(layer_out, mix_gain, placed, shard_count, capacity):
    features = layer_out.shape[1]
    feature_mean = jnp.mean(layer_out * layer_out, axis=1, keepdims=True)
    ready = (layer_out * lax.rsqrt(feature_mean + 1e-05) * mix_gain[None, :]).astype(jnp.bfloat16)
    return (
        jnp.zeros((shard_count * capacity, features), jnp.bfloat16)
        .at[placed]
        .set(ready)
        .reshape(shard_count, capacity, features)
    )


def general(
    events,
    w_gate,
    w_inner,
    w_bc,
    w_step,
    step_bias,
    log_decay,
    norm_gain,
    w_out,
    mix_gain,
    port,
    port_shard,
    w_up,
    b_up,
    w_down,
):
    length = events.shape[0]
    heads_here = w_step.shape[1]
    channels = w_inner.shape[1]
    head_dim = channels // heads_here
    nstate = w_bc.shape[1] // 2
    blocks = length // BLOCK
    gate_pre = jnp.dot(events, w_gate, preferred_element_type=jnp.float32)
    inner_pre = jnp.dot(events, w_inner, preferred_element_type=jnp.float32)
    bc_proj = jnp.dot(events, w_bc, preferred_element_type=jnp.float32).astype(jnp.bfloat16)
    step_size = jax.nn.softplus(
        jnp.dot(events, w_step, preferred_element_type=jnp.float32) + step_bias[None, :]
    )
    scaled = (inner_pre.reshape(length, heads_here, head_dim) * step_size[:, :, None]).astype(
        jnp.bfloat16
    )
    b_blocks = bc_proj[:, :nstate].reshape(blocks, BLOCK, nstate)
    c_blocks = bc_proj[:, nstate:].reshape(blocks, BLOCK, nstate)
    x_blocks = scaled.reshape(blocks, BLOCK, heads_here, head_dim).astype(jnp.float32)
    decay_blocks = log_decay.reshape(heads_here, blocks, BLOCK)
    running = jnp.cumsum(decay_blocks, axis=2)
    causal_mask = jnp.arange(BLOCK)[:, None] >= jnp.arange(BLOCK)[None, :]
    spread = running[:, :, :, None] - running[:, :, None, :]
    weights = jnp.where(causal_mask, jnp.exp(jnp.where(causal_mask, spread, 0.0)), 0.0)
    affinity = jnp.einsum("cin,cjn->cij", c_blocks, b_blocks, preferred_element_type=jnp.float32)
    mixing = affinity[None] * weights
    within = jnp.einsum("hcij,cjhp->cihp", mixing, x_blocks, precision=lax.Precision.HIGHEST)
    to_end = jnp.exp(running[:, :, -1:] - running)
    block_states = jnp.einsum(
        "cjn,hcj,cjhp->chnp",
        b_blocks.astype(jnp.float32),
        to_end,
        x_blocks,
        precision=lax.Precision.HIGHEST,
    )
    block_logs = running[:, :, -1]
    block_decay = jnp.exp(block_logs)
    entering = []
    running_state = jnp.zeros((heads_here, nstate, head_dim), jnp.float32)
    for block_index in range(blocks):
        entering.append(running_state)
        running_state = (
            block_decay[:, block_index][:, None, None] * running_state + block_states[block_index]
        )
    device_decay = jnp.prod(block_decay, axis=1)
    summary = (device_decay, running_state)
    identity = (jnp.ones_like(device_decay), jnp.zeros_like(running_state))
    carried = entering_2(summary, ("tm", "sub"), combine_states, identity)
    carry_state = carried[1]
    before_block = jnp.exp(jnp.cumsum(block_logs, axis=1) - block_logs)
    start_states = jnp.stack(entering) + before_block.T[:, :, None, None] * carry_state[None]
    from_state = jnp.einsum(
        "cin,hci,chnp->cihp",
        c_blocks.astype(jnp.float32),
        jnp.exp(running),
        start_states,
        precision=lax.Precision.HIGHEST,
    )
    ssm_out = (within + from_state).reshape(length, heads_here, head_dim)
    gated = ssm_out * jax.nn.silu(gate_pre.reshape(length, heads_here, head_dim))
    square_mean = jnp.mean(gated * gated, axis=2, keepdims=True)
    normed = (
        (gated * lax.rsqrt(square_mean + 1e-05) * norm_gain.reshape(heads_here, head_dim))
        .reshape(length, channels)
        .astype(jnp.bfloat16)
    )
    partial_sums = jnp.dot(normed, w_out, preferred_element_type=jnp.float32)
    shard_count = lax.axis_size("tm")
    capacity = 2 * length // shard_count
    port_table = port[:, None] == jnp.arange(port_shard.shape[0])[None, :]
    target = jnp.sum(jnp.where(port_table, port_shard[None, :], 0), axis=1)
    target_hot = (target[:, None] == jnp.arange(shard_count)[None, :]).astype(jnp.int32)
    slot_index = jnp.sum((jnp.cumsum(target_hot, axis=0) - 1) * target_hot, axis=1)
    placed = target * capacity + slot_index
    layer_out = lax.psum(partial_sums.astype(jnp.bfloat16), "mp").astype(jnp.float32)
    outgoing = place_rows(layer_out, mix_gain, placed, shard_count, capacity)
    received = lax.all_to_all(outgoing, "tm", split_axis=0, concat_axis=0, tiled=True)
    flat_rows = received.reshape(shard_count * capacity, received.shape[2])
    hidden_units = jax.nn.gelu(
        jnp.dot(flat_rows, w_up[0], preferred_element_type=jnp.float32) + b_up[0][None, :],
        approximate=True,
    ).astype(jnp.bfloat16)
    partial_out = jnp.dot(hidden_units, w_down[0], preferred_element_type=jnp.float32).reshape(
        shard_count, capacity, w_down.shape[2]
    )
    readout = lax.psum_scatter(
        partial_out.astype(jnp.bfloat16), "mp", scatter_dimension=2, tiled=True
    )
    returned = lax.all_to_all(readout, "tm", split_axis=0, concat_axis=0, tiled=True)
    return returned.reshape(shard_count * capacity, returned.shape[2])[placed]


SPAN = 128
TILE = 16
VMEM = pl.BlockSpec(memory_space=pltpu.VMEM)
SMEM = pl.BlockSpec(memory_space=pltpu.SMEM)
ANY = pl.BlockSpec(memory_space=pl.ANY)


def call(kernel, out_shape, *, micros, in_specs, after=(), room=24, **kw):
    count = len(in_specs)

    def body(*refs):
        kernel(*refs[:count], *refs[count + len(after) :])

    run = pl.pallas_call(
        body,
        in_specs=[*in_specs, *[ANY] * len(after)],
        out_shape=out_shape,
        cost_estimate=pl.CostEstimate(
            flops=int(micros * 1e9), bytes_accessed=int(micros * 3e6), transcendentals=0
        ),
        compiler_params=pltpu.CompilerParams(vmem_limit_bytes=room * 1024 * 1024),
        **kw,
    )
    return lambda *args: run(*args, *after)


def arr(shape, kind):
    return jax.ShapeDtypeStruct(shape, kind)


def dot(a, b, left=1, right=0):
    return lax.dot_general(a, b, (((left,), (right,)), ((), ())), preferred_element_type=F32)


def split(v, terms):
    out = []
    for _ in range(terms):
        part = v.astype(BF16)
        out.append(part)
        v = v - part.astype(F32)
    return out


def tie(x, first):
    return lax.optimization_barrier((x, first))[0]


def head_lanes(heads, channels):
    first = iota((heads, channels), 0) * (channels // heads)
    lane = iota((heads, channels), 1)
    return ones_where((lane >= first) & (lane < first + channels // heads))


def spread_heads(v, lanes):
    return sum(dot(part, lanes) for part in split(v, 2))


def iota(shape, dim):
    return lax.broadcasted_iota(jnp.int32, shape, dim)


def ones_where(mask, kind=BF16):
    return jnp.where(mask, 1.0, 0.0).astype(kind)


def scan_in_kernel(ev, w_inner, w_bc, w_step, bias, decay, scaled_o, bc_o, sum_o, state, total):
    step_id = pl.program_id(0)
    rows = ev.shape[0]
    nstate = w_bc.shape[1] // 2
    x = ev[...]
    lanes = head_lanes(decay.shape[0], w_inner.shape[1])
    inner = dot(x, w_inner[...])
    bc = dot(x, w_bc[...]).astype(BF16)
    pre = dot(x, w_step[...], 1, 1) + bias[...]
    step = jnp.maximum(pre, 0.0) + jnp.log1p(jnp.exp(-jnp.abs(pre)))
    scaled = (inner * spread_heads(step, lanes)).astype(BF16)
    scaled_o[...] = scaled
    bc_o[...] = bc
    logs = split(decay[...], 3)
    later = ones_where(iota((rows, rows), 1) > iota((rows, rows), 0))
    to_end = jnp.exp(sum(dot(later, part, 1, 1) for part in logs))
    whole = jnp.exp(sum(dot(jnp.ones((8, rows), BF16), part, 1, 1) for part in logs))
    weighted = (scaled.astype(F32) * spread_heads(to_end, lanes)).astype(BF16)
    fresh = dot(bc[:, :nstate], weighted, 0, 0)
    fade = spread_heads(whole, lanes)

    @pl.when(step_id == 0)
    def _():
        state[...] = fresh
        total[...] = fade

    @pl.when(step_id > 0)
    def _():
        state[...] = state[...] * fade[:1] + fresh
        total[...] = total[...] * fade

    @pl.when(step_id == pl.num_programs(0) - 1)
    def _():
        put_summary(sum_o, state[...], total[:1])


def put_summary(ref, state, decay):
    n, width = state.shape
    ref[:n, :] = state.astype(BF16)
    high = decay.astype(BF16).astype(F32)
    row = iota((TILE, width), 0)
    ref[n:, :] = jnp.where(row == 0, high, jnp.where(row == 1, decay - high, 0.0)).astype(BF16)


def get_summary(value):
    n = value.shape[0] - TILE
    value = value.astype(F32)
    return value[n : n + 1] + value[n + 1 : n + 2], value[:n]


def chip_kernel(info, own, other, out):
    half = out.shape[1]
    place = info[3]
    cols = pl.ds(pl.multiple_of(place * half, half), half)
    mine, theirs = own[:, cols].astype(F32), other[:, cols].astype(F32)
    first = jnp.where(place == 0, mine, theirs)
    second = jnp.where(place == 0, theirs, mine)
    decay_1, state_1 = get_summary(first)
    decay_2, state_2 = get_summary(second)
    put_summary(out, decay_2 * state_1 + state_2, decay_1 * decay_2)


def carry_kernel(*refs):
    out = refs[-1]
    state = None
    for ref in reversed(refs[:-1]):
        decay, fresh = get_summary(ref[...])
        state = fresh if state is None else decay * state + fresh
    out[...] = state.astype(BF16)


def within_kernel(scaled, bc, decay, y_o, past_o, state, run):
    step_id = pl.program_id(0)
    rows = scaled.shape[0]
    heads = decay.shape[0]
    nstate = bc.shape[1] // 2
    pair = scaled.shape[1] * 2 // heads

    @pl.when(step_id == 0)
    def _():
        state[...] = jnp.zeros_like(state)
        run[...] = jnp.zeros_like(run)

    lanes = head_lanes(heads, scaled.shape[1])
    halves = head_lanes(2, pair)
    row, col = iota((rows, rows), 0), iota((rows, rows), 1)
    causal = row >= col
    logs = split(decay[...], 3)
    until = sum(dot(ones_where(causal), part, 1, 1) for part in logs)
    until_row = sum(dot(part, ones_where(row <= col)) for part in logs)
    b, c = bc[:, :nstate], bc[:, nstate:]
    affinity = dot(c, b, 1, 1)
    past = spread_heads(jnp.exp(until), lanes) * dot(c, state[...].astype(BF16))
    for number in range(heads // 2):
        mixes = []
        for head in (2 * number, 2 * number + 1):
            gap = until[:, head : head + 1] - until_row[head : head + 1, :]
            mixes.append((affinity * jnp.exp(jnp.where(causal, gap, -1e30))).astype(BF16))
        cols = slice(number * pair, (number + 1) * pair)
        x = scaled[:, cols]
        both = jnp.concatenate([x * halves[0:1, :], x * halves[1:2, :]], axis=0)
        y_o[:, cols] = past[:, cols] + dot(jnp.concatenate(mixes, axis=1), both)
    last = until[rows - 1 :, :]
    weighted = scaled[...].astype(F32) * spread_heads(jnp.exp(last - until), lanes)
    fade = spread_heads(jnp.exp(jnp.broadcast_to(last, (8, heads))), lanes)
    state[...] = state[...] * fade[:1] + dot(b, weighted.astype(BF16), 0, 0)
    past_o[...] = jnp.exp(until + run[:1])
    run[...] += jnp.broadcast_to(last, run.shape)


def norm_kernel(info, y, gate, bc, past, mine, other, before, gain, w_out, slot, out, carry, all_rows):
    step_id = pl.program_id(0)
    rows, channels = y.shape
    heads = past.shape[1]
    nstate = bc.shape[1] // 2
    lanes = head_lanes(heads, channels)

    @pl.when(step_id == 0)
    def _():
        here = info[3]
        a, b = mine[...].astype(F32), other[...].astype(F32)
        low, high = jnp.where(here == 0, a, b), jnp.where(here == 0, b, a)
        chip = jnp.concatenate([low, high], axis=1)
        decay, state = get_summary(before[...])
        carry[...] = jnp.where(here == 0, chip, decay * chip + state).astype(BF16)

    ssm = y[...] + spread_heads(past[...], lanes) * dot(bc[:, nstate:], carry[...])
    gated = ssm * gate[...]
    square = dot((gated * gated).astype(BF16), lanes, 1, 1) * (heads / channels)
    scale = spread_heads(lax.rsqrt(square + 1e-05), lanes)
    normed = (gated * scale * gain[...][None, :]).astype(BF16)
    all_rows[pl.ds(pl.multiple_of(step_id * rows, rows), rows), :] = dot(normed, w_out[...]).astype(BF16)

    @pl.when(step_id == pl.num_programs(0) - 1)
    def _():
        count = out.shape[1]
        here = 2 * (info[0] & 1) + info[1]
        for place in range(4):
            first = (place ^ here) * count
            pick = ones_where(slot[...] == iota((count, slot.shape[1]), 0) + first)
            out[place] = dot(pick, all_rows[...]).astype(BF16)


def mixed(term_1, term_2, gain):
    total = term_1[...].astype(F32) + term_2[...].astype(F32)
    mean = jnp.mean(total * total, axis=1, keepdims=True)
    return (total * lax.rsqrt(mean + 1e-05) * gain[...][None, :]).astype(BF16)


def route_kernel(cold, info, shard, port, slot_o, column_o, flag_o):
    length = port.shape[1]
    half_rows = 2 * length // 4 // 2
    rows = half_rows + cold
    target = jnp.zeros(port.shape, jnp.int32)
    for number in range(shard.shape[0]):
        target = jnp.where(port[...] == number, shard[number], target)
    group = iota((8, length), 0)
    member = ones_where(jnp.broadcast_to(target, (8, length)) == group, F32)
    lane = iota((8, length), 1)
    count = member
    reach = 1
    while reach < length:
        count = count + jnp.where(lane >= reach, pltpu.roll(count, reach, 1), 0.0)
        reach *= 2
    rank = jnp.sum(member * (count - 1.0), axis=0, keepdims=True).astype(jnp.int32)
    whole = jnp.broadcast_to(count[:, length - 1 :], (8, 128))
    big = jnp.where(whole == 2.0 * half_rows, group[:, :128], 0)
    hot = jnp.max(big.astype(F32)).astype(jnp.int32)
    flag_o[0] = jnp.where(hot == info[0], 0, 1)
    away = target ^ info[0]
    half = (rank & 1) ^ info[1]
    row = rank >> 1
    row = jnp.where(away >= 2, rows - 1 - row, row)
    slot = (2 * (away & 1) + half) * rows + row
    slot_o[...] = slot
    wide = jnp.broadcast_to(slot.astype(F32), (128, length))
    column_o[...] = wide.T.astype(jnp.int32)


def readout_kernel(cold, info, flag, terms, gain, bias, w_up, w_down, *refs):
    pieces = refs[:10]
    same_o, other_o, same_l_o, other_l_o, up, down, extra, total, sems = refs[10:]
    width = up.shape[1]
    part = width // 4
    copies = [[] for _ in range(4)]
    used = 0

    def start(bank, source, target):
        nonlocal used
        copy = pltpu.make_async_copy(source, target, sems.at[used])
        copy.start()
        copies[bank].append(copy)
        used += 1

    start(0, w_up.at[0], up.at[0])
    start(0, w_down.at[0], down.at[0])
    for core in (0, 1):
        here = (info[3] ^ core) * 2
        at = pl.ds(pl.multiple_of(here * part, 2 * part), 2 * part)
        piece = pieces[5 * core]
        start(1, piece.at[pl.ds(0, 2 * part)], up.at[1, at])
        start(1, piece.at[pl.ds(2 * part, 2 * part)], down.at[1, at])
        for number, bank in enumerate((2, 2, 3, 3)):
            piece = pieces[5 * core + 1 + number]
            first = here + (info[2] ^ (number % 2))
            at = pl.ds(pl.multiple_of(first * part, part), part)
            start(bank, piece.at[pl.ds(0, part)], up.at[bank, at])
            start(bank, piece.at[pl.ds(part, part)], down.at[bank, at])
    start(1, pieces[0].at[pl.ds(4 * part, TILE)], extra.at[1])
    start(2, pieces[1].at[pl.ds(2 * part, TILE)], extra.at[2])
    start(3, pieces[3].at[pl.ds(2 * part, TILE)], extra.at[3])

    odd = info[0] & 1
    away = mixed(terms.at[2 - 2 * odd], terms.at[3 - 2 * odd], gain)
    local = mixed(terms.at[2 * odd], terms.at[2 * odd + 1], gain)
    count = away.shape[0]

    def run(lo, hi, bank, first):
        size = hi - lo
        x = jnp.concatenate([away[lo:hi], local[lo:hi]], axis=0)
        out = None
        for half in (0, 1):
            if first:
                for copy in copies[bank + half]:
                    copy.wait()
            if bank + half == 0:
                shift = bias[...]
            else:
                shift = jnp.sum(extra[bank + half].astype(F32), axis=0, keepdims=True)
            v = dot(x, up[bank + half]) + shift
            hidden = (0.5 * v * (1.0 + jnp.tanh(0.7978845608028654 * (v + 0.044715 * v * v * v)))).astype(BF16)
            y = dot(hidden, down[bank + half])
            out = y if half == 0 else out + y
        total[0, lo:hi, :] = out[:size]
        total[1, lo:hi, :] = out[size:]

    run(0, cold, 0, True)
    run(count - cold, count, 2, True)

    @pl.when(flag[0] == 0)
    def _():
        run(cold, count - cold, 0, False)

    @pl.when(flag[0] != 0)
    def _():
        run(cold, count - cold, 2, False)

    place = info[1]
    side = same_o.shape[1]
    for number, (near, far) in enumerate(((same_o, other_o), (same_l_o, other_l_o))):
        low, high = total[number, :, :side], total[number, :, side:]
        near[...] = jnp.where(place == 0, low, high).astype(BF16)
        far[...] = jnp.where(place == 0, high, low).astype(BF16)


def payload_kernel(info, bias, w_up, w_down, out, sems):
    part = (out.shape[0] - TILE) // 2
    first = info[3] * (out.shape[1] // 2)
    if 2 * part < out.shape[1] // 2 + part:
        first = first + info[2] * part
    at = pl.ds(pl.multiple_of(first, part), part)
    copies = [
        pltpu.make_async_copy(w.at[0, at], out.at[pl.ds(number * part, part)], sems.at[number])
        for number, w in enumerate((w_up, w_down))
    ]
    for copy in copies:
        copy.start()
    row = iota((TILE, out.shape[1]), 0)
    rows = jnp.zeros((TILE, out.shape[1]), F32)
    for number, term in enumerate(split(bias[...], 3)):
        rows = jnp.where(row == number, term.astype(F32), rows)
    out[2 * part :, :] = rows.astype(BF16)
    for copy in copies:
        copy.wait()


def gate_kernel(ev, w_gate, out):
    gate = dot(ev[...], w_gate[...])
    out[...] = gate / (1.0 + jnp.exp(-gate))


def collect_kernel(column, a, b, c, d, out, joined):
    rows = a.shape[0]

    @pl.when(pl.program_id(0) == 0)
    def _():
        for number, ref in enumerate((a, b, c, d)):
            joined[number * rows : (number + 1) * rows, :] = ref[...]

    place = column[...]
    lane = iota(place.shape, 1)
    picks = [ones_where(place == lane + first) for first in range(0, 4 * rows, 128)]
    out[...] = dot(jnp.concatenate(picks, axis=1), joined[...]).astype(BF16)


def hold(block, index):
    return pl.BlockSpec(block, index)


def fixed(shape):
    return pl.BlockSpec(shape, lambda i: (0,) * len(shape))


def fast(
    events,
    w_gate,
    w_inner,
    w_bc,
    w_step,
    step_bias,
    log_decay,
    norm_gain,
    w_out,
    mix_gain,
    port,
    port_shard,
    w_up,
    b_up,
    w_down,
):
    length, width = events.shape
    channels = w_inner.shape[1]
    heads = w_step.shape[1]
    head_dim = channels // heads
    nstate = w_bc.shape[1] // 2
    shard_count = lax.axis_size("tm")
    hot_rows = 2 * length // shard_count // 2
    most = -(-(length - 2 * hot_rows) // (shard_count - 1))
    cold = -(-((most + 1) // 2) // TILE) * TILE
    count = hot_rows + cold
    info = jnp.stack([lax.axis_index(a) for a in ("tm", "mp", "groups", "sub")]).astype(jnp.int32)
    swap = [(0, 1), (1, 0)]
    side = width // 2

    part = width // 4
    def payload(rows, room, after):
        return call(
            payload_kernel,
            arr((2 * rows + TILE, width), BF16),
            micros=0.1,
            room=room,
            in_specs=[SMEM, VMEM, ANY, ANY],
            out_specs=VMEM,
            scratch_shapes=[pltpu.SemaphoreType.DMA((2,))],
            after=after,
        )(info, b_up, w_up, w_down)

    share = payload(part, 62, ())
    far = lax.ppermute(share, "tm", [(i, i ^ 2) for i in range(shard_count)])

    rows = 2 * SPAN
    grid = (length // rows,)
    scaled, bc, summary = call(
        scan_in_kernel,
        (
            arr((length, channels), BF16),
            arr((length, 2 * nstate), BF16),
            arr((nstate + TILE, channels), BF16),
        ),
        room=62,
        after=(share,),
        micros=0.1,
        grid=grid,
        in_specs=[
            hold((rows, width), lambda i: (i, 0)),
            fixed(w_inner.shape),
            fixed(w_bc.shape),
            fixed((heads, width)),
            fixed((1, heads)),
            hold((heads, rows), lambda i: (0, i)),
        ],
        out_specs=(
            hold((rows, channels), lambda i: (i, 0)),
            hold((rows, 2 * nstate), lambda i: (i, 0)),
            fixed((nstate + TILE, channels)),
        ),
        scratch_shapes=[pltpu.VMEM((nstate, channels), F32), pltpu.VMEM((8, channels), F32)],
    )(events, w_inner, w_bc, w_step.T, step_bias[None, :], log_decay)
    beside = lax.ppermute(summary, "sub", swap)
    chip = call(
        chip_kernel,
        arr((nstate + TILE, channels // 2), BF16),
        micros=0.1,
        in_specs=[SMEM, VMEM, VMEM],
        out_specs=VMEM,
    )(info, summary, beside)
    earlier = [
        lax.ppermute(chip, "tm", [(i, i + hop) for i in range(shard_count - hop)])
        for hop in range(1, shard_count)
    ]

    own = lax.ppermute(payload(2 * part, 24, (summary,)), "mp", swap)
    slot, column, flag = call(
        lambda *refs: route_kernel(cold, *refs),
        (arr((1, length), jnp.int32), arr((length, 128), jnp.int32), arr((1,), jnp.int32)),
        micros=0.1,
        in_specs=[SMEM, SMEM, VMEM],
        out_specs=(VMEM, VMEM, SMEM),
    )(info, port_shard, port[None, :])
    gate = call(
        gate_kernel,
        arr((length, channels), F32),
        room=24,
        micros=0.1,
        grid=grid,
        in_specs=[hold((rows, width), lambda i: (i, 0)), fixed(w_gate.shape)],
        out_specs=hold((rows, channels), lambda i: (i, 0)),
        after=(chip, slot),
    )(events, w_gate)
    y, past = call(
        within_kernel,
        (arr((length, channels), F32), arr((length, heads), F32)),
        room=24,
        micros=2.0,
        grid=(length // SPAN,),
        in_specs=[
            hold((SPAN, channels), lambda i: (i, 0)),
            hold((SPAN, 2 * nstate), lambda i: (i, 0)),
            hold((heads, SPAN), lambda i: (0, i)),
        ],
        out_specs=(
            hold((SPAN, channels), lambda i: (i, 0)),
            hold((SPAN, heads), lambda i: (i, 0)),
        ),
        scratch_shapes=[pltpu.VMEM((nstate, channels), F32), pltpu.VMEM((8, heads), F32)],
        after=(gate,),
    )(scaled, bc, log_decay)

    carry = call(
        carry_kernel,
        arr((nstate, channels // 2), BF16),
        micros=0.1,
        in_specs=[VMEM] * len(earlier),
        out_specs=VMEM,
        after=(past, slot, far),
    )(*earlier)
    far = tie(far, carry)
    far_x = lax.ppermute(far, "mp", swap)
    far_y = lax.ppermute(far, "groups", swap)
    carry_beside = lax.ppermute(carry, "sub", swap)

    blocks = call(
        norm_kernel,
        arr((4, count, width), BF16),
        room=24,
        micros=0.1,
        grid=grid,
        in_specs=[
            SMEM,
            hold((rows, channels), lambda i: (i, 0)),
            hold((rows, channels), lambda i: (i, 0)),
            hold((rows, 2 * nstate), lambda i: (i, 0)),
            hold((rows, heads), lambda i: (i, 0)),
            fixed(carry.shape),
            fixed(carry.shape),
            fixed(beside.shape),
            fixed((channels,)),
            fixed(w_out.shape),
            fixed(slot.shape),
        ],
        out_specs=fixed((4, count, width)),
        scratch_shapes=[pltpu.VMEM((nstate, channels), BF16), pltpu.VMEM((length, width), BF16)],
    )(info, y, gate, bc, past, carry, carry_beside, beside, norm_gain, w_out, slot)
    near = [(i, i ^ 1) for i in range(shard_count)]
    near_x = [(2 * i + j, 2 * (i ^ 1) + (j ^ 1)) for i in range(shard_count) for j in range(2)]
    squares = [[4 * i + j for j in range(4)] for i in range(shard_count // 2)]
    blocks = tie(tie(tie(blocks, far_x), far_y), own)
    terms = lax.all_to_all(
        blocks, ("tm", "mp"), 0, 0, axis_index_groups=squares, tiled=True
    )
    own, far, far_y, far_x = (tie(a, blocks) for a in (own, far, far_y, far_x))
    far_xy = lax.ppermute(far_x, "groups", swap)
    firsts = [own, far, far_y, far_x, far_xy]
    pieces = firsts + [lax.ppermute(a, "sub", swap) for a in firsts]

    same, other, same_l, other_l = call(
        lambda *refs: readout_kernel(cold, *refs),
        (arr((count, side), BF16),) * 4,
        room=60,
        micros=1,
        in_specs=[SMEM, SMEM] + [VMEM] * 3 + [ANY] * 12,
        out_specs=(VMEM,) * 4,
        scratch_shapes=[
            pltpu.VMEM((4, width, width), BF16),
            pltpu.VMEM((4, width, width), BF16),
            pltpu.VMEM((4, TILE, width), BF16),
            pltpu.VMEM((2, count, width), F32),
            pltpu.SemaphoreType.DMA((29,)),
        ],
    )(info, flag, terms, mix_gain, b_up, w_up, w_down, *pieces)
    back_same = lax.ppermute(same, "tm", near)
    back_other = lax.ppermute(other, ("tm", "mp"), near_x)
    back_l = lax.ppermute(other_l, "mp", swap)

    return call(
        collect_kernel,
        arr((length, side), BF16),
        micros=1,
        grid=grid,
        in_specs=[hold((rows, 128), lambda i: (i, 0))] + [fixed((count, side))] * 4,
        out_specs=hold((rows, side), lambda i: (i, 0)),
        scratch_shapes=[pltpu.VMEM((4 * count, side), BF16)],
    )(column, same_l, back_l, back_same, back_other)


def shards(*args):
    events, w_inner, w_step = args[0], args[2], args[4]
    sizes = tuple(lax.axis_size(a) for a in ("groups", "tm", "mp", "sub"))
    heads = w_step.shape[1]
    square = events.shape[1] == w_inner.shape[1] == args[12].shape[2]
    if sizes == (2, 4, 2, 2) and heads % 4 == 0 and square and events.shape[0] % 512 == 0:
        return fast(*args)
    return general(*args)


def solution(mesh):
    in_specs = (
        P(("groups", "tm", "sub"), None),
        P(None, "mp"),
        P(None, "mp"),
        P(),
        P(None, "mp"),
        P("mp"),
        P("mp", ("groups", "tm", "sub")),
        P("mp"),
        P("mp", None),
        P(),
        P(("groups", "tm", "sub")),
        P("groups"),
        P("tm", None, "mp"),
        P("tm", "mp"),
        P("tm", "mp", None),
    )
    out_specs = P(("groups", "tm", "sub"), "mp")
    return jax.shard_map(shards, mesh=mesh, in_specs=in_specs, out_specs=out_specs, check_vma=False)
```

```python
import jax
import jax.numpy as jnp
from jax import lax
from jax.experimental import pallas as pl
from jax.experimental.pallas import tpu as pltpu
from jax.sharding import PartitionSpec as P

BLOCK = 256
F32 = jnp.float32
BF16 = jnp.bfloat16


def entering_2(shard, axis, join, neutral):
    place = lax.axis_index(axis)
    gathered = jax.tree.map(
        lambda a, kind: lax.all_gather(a.astype(kind), axis),
        shard,
        jax.tree.map(lambda a: jnp.bfloat16 if a.dtype == jnp.float32 else a.dtype, shard),
    )
    state = jax.tree.map(lambda a, e: jnp.zeros_like(a) + jnp.asarray(e, a.dtype), shard, neutral)

    def one(hop, state):
        return join(
            state,
            jax.tree.map(
                lambda a, own: lax.dynamic_index_in_dim(a, hop, 0, False).astype(own.dtype),
                gathered,
                shard,
            ),
        )

    return lax.fori_loop(0, place, one, state)


def combine_states(earlier, later):
    decay_early, state_early = earlier
    decay_late, state_late = later
    return (decay_early * decay_late, decay_late[:, None, None] * state_early + state_late)


def place_rows(layer_out, mix_gain, placed, shard_count, capacity):
    features = layer_out.shape[1]
    feature_mean = jnp.mean(layer_out * layer_out, axis=1, keepdims=True)
    ready = (layer_out * lax.rsqrt(feature_mean + 1e-05) * mix_gain[None, :]).astype(jnp.bfloat16)
    return (
        jnp.zeros((shard_count * capacity, features), jnp.bfloat16)
        .at[placed]
        .set(ready)
        .reshape(shard_count, capacity, features)
    )


def general(
    events,
    w_gate,
    w_inner,
    w_bc,
    w_step,
    step_bias,
    log_decay,
    norm_gain,
    w_out,
    mix_gain,
    port,
    port_shard,
    w_up,
    b_up,
    w_down,
):
    length = events.shape[0]
    heads_here = w_step.shape[1]
    channels = w_inner.shape[1]
    head_dim = channels // heads_here
    nstate = w_bc.shape[1] // 2
    blocks = length // BLOCK
    gate_pre = jnp.dot(events, w_gate, preferred_element_type=jnp.float32)
    inner_pre = jnp.dot(events, w_inner, preferred_element_type=jnp.float32)
    bc_proj = jnp.dot(events, w_bc, preferred_element_type=jnp.float32).astype(jnp.bfloat16)
    step_size = jax.nn.softplus(
        jnp.dot(events, w_step, preferred_element_type=jnp.float32) + step_bias[None, :]
    )
    scaled = (inner_pre.reshape(length, heads_here, head_dim) * step_size[:, :, None]).astype(
        jnp.bfloat16
    )
    b_blocks = bc_proj[:, :nstate].reshape(blocks, BLOCK, nstate)
    c_blocks = bc_proj[:, nstate:].reshape(blocks, BLOCK, nstate)
    x_blocks = scaled.reshape(blocks, BLOCK, heads_here, head_dim).astype(jnp.float32)
    decay_blocks = log_decay.reshape(heads_here, blocks, BLOCK)
    running = jnp.cumsum(decay_blocks, axis=2)
    causal_mask = jnp.arange(BLOCK)[:, None] >= jnp.arange(BLOCK)[None, :]
    spread = running[:, :, :, None] - running[:, :, None, :]
    weights = jnp.where(causal_mask, jnp.exp(jnp.where(causal_mask, spread, 0.0)), 0.0)
    affinity = jnp.einsum("cin,cjn->cij", c_blocks, b_blocks, preferred_element_type=jnp.float32)
    mixing = affinity[None] * weights
    within = jnp.einsum("hcij,cjhp->cihp", mixing, x_blocks, precision=lax.Precision.HIGHEST)
    to_end = jnp.exp(running[:, :, -1:] - running)
    block_states = jnp.einsum(
        "cjn,hcj,cjhp->chnp",
        b_blocks.astype(jnp.float32),
        to_end,
        x_blocks,
        precision=lax.Precision.HIGHEST,
    )
    block_logs = running[:, :, -1]
    block_decay = jnp.exp(block_logs)
    entering = []
    running_state = jnp.zeros((heads_here, nstate, head_dim), jnp.float32)
    for block_index in range(blocks):
        entering.append(running_state)
        running_state = (
            block_decay[:, block_index][:, None, None] * running_state + block_states[block_index]
        )
    device_decay = jnp.prod(block_decay, axis=1)
    summary = (device_decay, running_state)
    identity = (jnp.ones_like(device_decay), jnp.zeros_like(running_state))
    carried = entering_2(summary, ("tm", "sub"), combine_states, identity)
    carry_state = carried[1]
    before_block = jnp.exp(jnp.cumsum(block_logs, axis=1) - block_logs)
    start_states = jnp.stack(entering) + before_block.T[:, :, None, None] * carry_state[None]
    from_state = jnp.einsum(
        "cin,hci,chnp->cihp",
        c_blocks.astype(jnp.float32),
        jnp.exp(running),
        start_states,
        precision=lax.Precision.HIGHEST,
    )
    ssm_out = (within + from_state).reshape(length, heads_here, head_dim)
    gated = ssm_out * jax.nn.silu(gate_pre.reshape(length, heads_here, head_dim))
    square_mean = jnp.mean(gated * gated, axis=2, keepdims=True)
    normed = (
        (gated * lax.rsqrt(square_mean + 1e-05) * norm_gain.reshape(heads_here, head_dim))
        .reshape(length, channels)
        .astype(jnp.bfloat16)
    )
    partial_sums = jnp.dot(normed, w_out, preferred_element_type=jnp.float32)
    shard_count = lax.axis_size("tm")
    capacity = 2 * length // shard_count
    port_table = port[:, None] == jnp.arange(port_shard.shape[0])[None, :]
    target = jnp.sum(jnp.where(port_table, port_shard[None, :], 0), axis=1)
    target_hot = (target[:, None] == jnp.arange(shard_count)[None, :]).astype(jnp.int32)
    slot_index = jnp.sum((jnp.cumsum(target_hot, axis=0) - 1) * target_hot, axis=1)
    placed = target * capacity + slot_index
    layer_out = lax.psum(partial_sums.astype(jnp.bfloat16), "mp").astype(jnp.float32)
    outgoing = place_rows(layer_out, mix_gain, placed, shard_count, capacity)
    received = lax.all_to_all(outgoing, "tm", split_axis=0, concat_axis=0, tiled=True)
    flat_rows = received.reshape(shard_count * capacity, received.shape[2])
    hidden_units = jax.nn.gelu(
        jnp.dot(flat_rows, w_up[0], preferred_element_type=jnp.float32) + b_up[0][None, :],
        approximate=True,
    ).astype(jnp.bfloat16)
    partial_out = jnp.dot(hidden_units, w_down[0], preferred_element_type=jnp.float32).reshape(
        shard_count, capacity, w_down.shape[2]
    )
    readout = lax.psum_scatter(
        partial_out.astype(jnp.bfloat16), "mp", scatter_dimension=2, tiled=True
    )
    returned = lax.all_to_all(readout, "tm", split_axis=0, concat_axis=0, tiled=True)
    return returned.reshape(shard_count * capacity, returned.shape[2])[placed]


SPAN = 128
TILE = 16
VMEM = pl.BlockSpec(memory_space=pltpu.VMEM)
SMEM = pl.BlockSpec(memory_space=pltpu.SMEM)
ANY = pl.BlockSpec(memory_space=pl.ANY)


def call(kernel, out_shape, *, micros, in_specs, after=(), room=24, **kw):
    count = len(in_specs)

    def body(*refs):
        kernel(*refs[:count], *refs[count + len(after) :])

    run = pl.pallas_call(
        body,
        in_specs=[*in_specs, *[ANY] * len(after)],
        out_shape=out_shape,
        cost_estimate=pl.CostEstimate(
            flops=int(micros * 1e9), bytes_accessed=int(micros * 3e6), transcendentals=0
        ),
        compiler_params=pltpu.CompilerParams(vmem_limit_bytes=room * 1024 * 1024),
        **kw,
    )
    return lambda *args: run(*args, *after)


def arr(shape, kind):
    return jax.ShapeDtypeStruct(shape, kind)


def dot(a, b, left=1, right=0):
    return lax.dot_general(a, b, (((left,), (right,)), ((), ())), preferred_element_type=F32)


def split(v, terms):
    out = []
    for _ in range(terms):
        part = v.astype(BF16)
        out.append(part)
        v = v - part.astype(F32)
    return out


def tie(x, first):
    return lax.optimization_barrier((x, first))[0]


def head_lanes(heads, channels):
    first = iota((heads, channels), 0) * (channels // heads)
    lane = iota((heads, channels), 1)
    return ones_where((lane >= first) & (lane < first + channels // heads))


def spread_heads(v, lanes):
    return sum(dot(part, lanes) for part in split(v, 2))


def iota(shape, dim):
    return lax.broadcasted_iota(jnp.int32, shape, dim)


def ones_where(mask, kind=BF16):
    return jnp.where(mask, 1.0, 0.0).astype(kind)


def scan_in_kernel(ev, w_inner, w_bc, w_step, bias, decay, scaled_o, bc_o, sum_o, state, total):
    step_id = pl.program_id(0)
    rows = ev.shape[0]
    nstate = w_bc.shape[1] // 2
    x = ev[...]
    lanes = head_lanes(decay.shape[0], w_inner.shape[1])
    inner = dot(x, w_inner[...])
    bc = dot(x, w_bc[...]).astype(BF16)
    pre = dot(x, w_step[...], 1, 1) + bias[...]
    step = jnp.maximum(pre, 0.0) + jnp.log1p(jnp.exp(-jnp.abs(pre)))
    scaled = (inner * spread_heads(step, lanes)).astype(BF16)
    scaled_o[...] = scaled
    bc_o[...] = bc
    logs = split(decay[...], 3)
    later = ones_where(iota((rows, rows), 1) > iota((rows, rows), 0))
    to_end = jnp.exp(sum(dot(later, part, 1, 1) for part in logs))
    whole = jnp.exp(sum(dot(jnp.ones((8, rows), BF16), part, 1, 1) for part in logs))
    weighted = (scaled.astype(F32) * spread_heads(to_end, lanes)).astype(BF16)
    fresh = dot(bc[:, :nstate], weighted, 0, 0)
    fade = spread_heads(whole, lanes)

    @pl.when(step_id == 0)
    def _():
        state[...] = fresh
        total[...] = fade

    @pl.when(step_id > 0)
    def _():
        state[...] = state[...] * fade[:1] + fresh
        total[...] = total[...] * fade

    @pl.when(step_id == pl.num_programs(0) - 1)
    def _():
        put_summary(sum_o, state[...], total[:1])


def put_summary(ref, state, decay):
    n, width = state.shape
    ref[:n, :] = state.astype(BF16)
    high = decay.astype(BF16).astype(F32)
    row = iota((TILE, width), 0)
    ref[n:, :] = jnp.where(row == 0, high, jnp.where(row == 1, decay - high, 0.0)).astype(BF16)


def get_summary(value):
    n = value.shape[0] - TILE
    value = value.astype(F32)
    return value[n : n + 1] + value[n + 1 : n + 2], value[:n]


def chip_kernel(info, own, other, out):
    half = out.shape[1]
    place = info[3]
    cols = pl.ds(pl.multiple_of(place * half, half), half)
    mine, theirs = own[:, cols].astype(F32), other[:, cols].astype(F32)
    first = jnp.where(place == 0, mine, theirs)
    second = jnp.where(place == 0, theirs, mine)
    decay_1, state_1 = get_summary(first)
    decay_2, state_2 = get_summary(second)
    put_summary(out, decay_2 * state_1 + state_2, decay_1 * decay_2)


def carry_kernel(*refs):
    out = refs[-1]
    state = None
    for ref in reversed(refs[:-1]):
        decay, fresh = get_summary(ref[...])
        state = fresh if state is None else decay * state + fresh
    out[...] = state.astype(BF16)


def within_kernel(scaled, bc, decay, y_o, past_o, state, run):
    step_id = pl.program_id(0)
    rows = scaled.shape[0]
    heads = decay.shape[0]
    nstate = bc.shape[1] // 2
    pair = scaled.shape[1] * 2 // heads

    @pl.when(step_id == 0)
    def _():
        state[...] = jnp.zeros_like(state)
        run[...] = jnp.zeros_like(run)

    lanes = head_lanes(heads, scaled.shape[1])
    halves = head_lanes(2, pair)
    row, col = iota((rows, rows), 0), iota((rows, rows), 1)
    causal = row >= col
    logs = split(decay[...], 3)
    until = sum(dot(ones_where(causal), part, 1, 1) for part in logs)
    until_row = sum(dot(part, ones_where(row <= col)) for part in logs)
    b, c = bc[:, :nstate], bc[:, nstate:]
    affinity = dot(c, b, 1, 1)
    past = spread_heads(jnp.exp(until), lanes) * dot(c, state[...].astype(BF16))
    for number in range(heads // 2):
        mixes = []
        for head in (2 * number, 2 * number + 1):
            gap = until[:, head : head + 1] - until_row[head : head + 1, :]
            mixes.append((affinity * jnp.exp(jnp.where(causal, gap, -1e30))).astype(BF16))
        cols = slice(number * pair, (number + 1) * pair)
        x = scaled[:, cols]
        both = jnp.concatenate([x * halves[0:1, :], x * halves[1:2, :]], axis=0)
        y_o[:, cols] = past[:, cols] + dot(jnp.concatenate(mixes, axis=1), both)
    last = until[rows - 1 :, :]
    weighted = scaled[...].astype(F32) * spread_heads(jnp.exp(last - until), lanes)
    fade = spread_heads(jnp.exp(jnp.broadcast_to(last, (8, heads))), lanes)
    state[...] = state[...] * fade[:1] + dot(b, weighted.astype(BF16), 0, 0)
    past_o[...] = jnp.exp(until + run[:1])
    run[...] += jnp.broadcast_to(last, run.shape)


def norm_kernel(info, y, gate, bc, past, mine, other, before, gain, w_out, slot, *refs):
    outs, (carry, all_rows) = refs[:4], refs[4:]
    step_id = pl.program_id(0)
    rows, channels = y.shape
    heads = past.shape[1]
    nstate = bc.shape[1] // 2
    lanes = head_lanes(heads, channels)

    @pl.when(step_id == 0)
    def _():
        here = info[3]
        a, b = mine[...].astype(F32), other[...].astype(F32)
        low, high = jnp.where(here == 0, a, b), jnp.where(here == 0, b, a)
        chip = jnp.concatenate([low, high], axis=1)
        decay, state = get_summary(before[...])
        carry[...] = jnp.where(here == 0, chip, decay * chip + state).astype(BF16)

    ssm = y[...] + spread_heads(past[...], lanes) * dot(bc[:, nstate:], carry[...])
    gated = ssm * gate[...]
    square = dot((gated * gated).astype(BF16), lanes, 1, 1) * (heads / channels)
    scale = spread_heads(lax.rsqrt(square + 1e-05), lanes)
    normed = (gated * scale * gain[...][None, :]).astype(BF16)
    all_rows[pl.ds(pl.multiple_of(step_id * rows, rows), rows), :] = dot(normed, w_out[...]).astype(BF16)

    @pl.when(step_id == pl.num_programs(0) - 1)
    def _():
        for number, out in enumerate(outs):
            count = out.shape[0]
            pick = ones_where(slot[...] == iota((count, slot.shape[1]), 0) + number * count)
            out[...] = dot(pick, all_rows[...]).astype(BF16)


def mixed(term_1, term_2, gain):
    total = term_1[...].astype(F32) + term_2[...].astype(F32)
    mean = jnp.mean(total * total, axis=1, keepdims=True)
    return (total * lax.rsqrt(mean + 1e-05) * gain[...][None, :]).astype(BF16)


def mix_kernel(keep, recv, term_1, term_2, gain, away, local):
    away[...] = mixed(term_1, term_2, gain)
    local[...] = mixed(keep, recv, gain)


def route_kernel(cold, info, shard, port, slot_o, column_o, flag_o):
    length = port.shape[1]
    half_rows = 2 * length // 4 // 2
    rows = half_rows + cold
    target = jnp.zeros(port.shape, jnp.int32)
    for number in range(shard.shape[0]):
        target = jnp.where(port[...] == number, shard[number], target)
    group = iota((8, length), 0)
    member = ones_where(jnp.broadcast_to(target, (8, length)) == group, F32)
    lane = iota((8, length), 1)
    count = member
    reach = 1
    while reach < length:
        count = count + jnp.where(lane >= reach, pltpu.roll(count, reach, 1), 0.0)
        reach *= 2
    rank = jnp.sum(member * (count - 1.0), axis=0, keepdims=True).astype(jnp.int32)
    whole = jnp.broadcast_to(count[:, length - 1 :], (8, 128))
    big = jnp.where(whole == 2.0 * half_rows, group[:, :128], 0)
    hot = jnp.max(big.astype(F32)).astype(jnp.int32)
    flag_o[0] = jnp.where(hot == info[0], 0, 1)
    away = target ^ info[0]
    half = (rank & 1) ^ info[1]
    row = rank >> 1
    row = jnp.where(away >= 2, rows - 1 - row, row)
    slot = (2 * (away & 1) + half) * rows + row
    slot_o[...] = slot
    wide = jnp.broadcast_to(slot.astype(F32), (128, length))
    column_o[...] = wide.T.astype(jnp.int32)


def starter(sems):
    copies = []

    def start(source, target):
        copies.append(pltpu.make_async_copy(source, target, sems.at[len(copies)]))
        copies[-1].start()

    return copies, start


def quarters(info, pieces, start, up, down, bank):
    part = up.shape[1] // 4
    for number, piece in enumerate(pieces):
        first = (info[3] ^ (number // 2)) * 2 + (info[2] ^ (number % 2))
        at = pl.ds(pl.multiple_of(first * part, part), part)
        start(piece.at[pl.ds(0, part)], up.at[bank, at])
        start(piece.at[pl.ds(part, part)], down.at[bank, at])


def weights_kernel(info, bias, w_up, w_down, own, own_s, far_1, far_2, far_1s, far_2s, up, down, shift, extra, sems):
    part = up.shape[1] // 4
    copies, start = starter(sems)
    start(w_up.at[0], up.at[0])
    start(w_down.at[0], down.at[0])
    for core, piece in enumerate((own, own_s)):
        at = pl.ds(pl.multiple_of((info[3] ^ core) * 2 * part, 2 * part), 2 * part)
        start(piece.at[pl.ds(0, 2 * part)], up.at[1, at])
        start(piece.at[pl.ds(2 * part, 2 * part)], down.at[1, at])
    quarters(info, (far_1, far_2, far_1s, far_2s), start, up, down, 2)
    start(own.at[pl.ds(4 * part, TILE)], extra.at[0])
    start(far_1.at[pl.ds(2 * part, TILE)], extra.at[1])
    for copy in copies:
        copy.wait()
    rows = [bias[...]] + [jnp.sum(extra[i].astype(F32), axis=0, keepdims=True) for i in range(2)]
    shift[...] = jnp.concatenate(rows + rows[:1], axis=0)


def readout_kernel(cold, info, flag, away, local, shift, up, down, *refs):
    pieces = refs[:4]
    same_o, other_o, same_l_o, other_l_o, total, up_3, down_3, extra, sems = refs[4:]
    copies, start = starter(sems)
    quarters(info, pieces, start, up_3, down_3, 0)
    start(pieces[0].at[pl.ds(up.shape[1] // 2, TILE)], extra)
    count = away.shape[0]

    def run(lo, hi, bank):
        size = hi - lo
        x = jnp.concatenate([away[lo:hi], local[lo:hi]], axis=0)
        out = None
        for half in (0, 1):
            if bank + half == 3:
                for copy in copies:
                    copy.wait()
                v = dot(x, up_3[0]) + jnp.sum(extra[...].astype(F32), axis=0, keepdims=True)
            else:
                v = dot(x, up[bank + half]) + shift[bank + half : bank + half + 1, :]
            hidden = (0.5 * v * (1.0 + jnp.tanh(0.7978845608028654 * (v + 0.044715 * v * v * v)))).astype(BF16)
            y = dot(hidden, down_3[0] if bank + half == 3 else down[bank + half])
            out = y if half == 0 else out + y
        total[0, lo:hi, :] = out[:size]
        total[1, lo:hi, :] = out[size:]

    @pl.when(flag[0] == 0)
    def _():
        run(0, count - cold, 0)
        run(count - cold, count, 2)

    @pl.when(flag[0] != 0)
    def _():
        run(0, cold, 0)
        run(cold, count, 2)

    place = info[1]
    side = same_o.shape[1]
    for number, (near, far) in enumerate(((same_o, other_o), (same_l_o, other_l_o))):
        low, high = total[number, :, :side], total[number, :, side:]
        near[...] = jnp.where(place == 0, low, high).astype(BF16)
        far[...] = jnp.where(place == 0, high, low).astype(BF16)


def payload_kernel(info, bias, w_up, w_down, out, sems):
    part = (out.shape[0] - TILE) // 2
    first = info[3] * (out.shape[1] // 2)
    if 2 * part < out.shape[1] // 2 + part:
        first = first + info[2] * part
    at = pl.ds(pl.multiple_of(first, part), part)
    copies = [
        pltpu.make_async_copy(w.at[0, at], out.at[pl.ds(number * part, part)], sems.at[number])
        for number, w in enumerate((w_up, w_down))
    ]
    for copy in copies:
        copy.start()
    row = iota((TILE, out.shape[1]), 0)
    rows = jnp.zeros((TILE, out.shape[1]), F32)
    for number, term in enumerate(split(bias[...], 3)):
        rows = jnp.where(row == number, term.astype(F32), rows)
    out[2 * part :, :] = rows.astype(BF16)
    for copy in copies:
        copy.wait()


def gate_kernel(ev, w_gate, out):
    gate = dot(ev[...], w_gate[...])
    out[...] = gate / (1.0 + jnp.exp(-gate))


def collect_kernel(column, a, b, c, d, out, joined):
    rows = a.shape[0]

    @pl.when(pl.program_id(0) == 0)
    def _():
        for number, ref in enumerate((a, b, c, d)):
            joined[number * rows : (number + 1) * rows, :] = ref[...]

    place = column[...]
    lane = iota(place.shape, 1)
    picks = [ones_where(place == lane + first) for first in range(0, 4 * rows, 128)]
    out[...] = dot(jnp.concatenate(picks, axis=1), joined[...]).astype(BF16)


def hold(block, index):
    return pl.BlockSpec(block, index)


def fixed(shape):
    return pl.BlockSpec(shape, lambda i: (0,) * len(shape))


def fast(
    events,
    w_gate,
    w_inner,
    w_bc,
    w_step,
    step_bias,
    log_decay,
    norm_gain,
    w_out,
    mix_gain,
    port,
    port_shard,
    w_up,
    b_up,
    w_down,
):
    length, width = events.shape
    channels = w_inner.shape[1]
    heads = w_step.shape[1]
    head_dim = channels // heads
    nstate = w_bc.shape[1] // 2
    shard_count = lax.axis_size("tm")
    hot_rows = 2 * length // shard_count // 2
    most = -(-(length - 2 * hot_rows) // (shard_count - 1))
    cold = -(-((most + 1) // 2) // TILE) * TILE
    count = hot_rows + cold
    info = jnp.stack([lax.axis_index(a) for a in ("tm", "mp", "groups", "sub")]).astype(jnp.int32)
    swap = [(0, 1), (1, 0)]
    side = width // 2

    part = width // 4
    def payload(rows, room, after):
        return call(
            payload_kernel,
            arr((2 * rows + TILE, width), BF16),
            micros=0.1,
            room=room,
            in_specs=[SMEM, VMEM, ANY, ANY],
            out_specs=VMEM,
            scratch_shapes=[pltpu.SemaphoreType.DMA((2,))],
            after=after,
        )(info, b_up, w_up, w_down)

    share = payload(part, 62, ())
    far = lax.ppermute(share, "tm", [(i, i ^ 2) for i in range(shard_count)])

    rows = 2 * SPAN
    grid = (length // rows,)
    scaled, bc, summary = call(
        scan_in_kernel,
        (
            arr((length, channels), BF16),
            arr((length, 2 * nstate), BF16),
            arr((nstate + TILE, channels), BF16),
        ),
        room=62,
        after=(share,),
        micros=0.1,
        grid=grid,
        in_specs=[
            hold((rows, width), lambda i: (i, 0)),
            fixed(w_inner.shape),
            fixed(w_bc.shape),
            fixed((heads, width)),
            fixed((1, heads)),
            hold((heads, rows), lambda i: (0, i)),
        ],
        out_specs=(
            hold((rows, channels), lambda i: (i, 0)),
            hold((rows, 2 * nstate), lambda i: (i, 0)),
            fixed((nstate + TILE, channels)),
        ),
        scratch_shapes=[pltpu.VMEM((nstate, channels), F32), pltpu.VMEM((8, channels), F32)],
    )(events, w_inner, w_bc, w_step.T, step_bias[None, :], log_decay)
    beside = lax.ppermute(summary, "sub", swap)
    chip = call(
        chip_kernel,
        arr((nstate + TILE, channels // 2), BF16),
        micros=0.1,
        in_specs=[SMEM, VMEM, VMEM],
        out_specs=VMEM,
    )(info, summary, beside)
    earlier = [
        lax.ppermute(chip, "tm", [(i, i + hop) for i in range(shard_count - hop)])
        for hop in range(1, shard_count)
    ]

    own = lax.ppermute(payload(2 * part, 24, (summary,)), "mp", swap)
    slot, column, flag = call(
        lambda *refs: route_kernel(cold, *refs),
        (arr((1, length), jnp.int32), arr((length, 128), jnp.int32), arr((1,), jnp.int32)),
        micros=0.1,
        in_specs=[SMEM, SMEM, VMEM],
        out_specs=(VMEM, VMEM, SMEM),
    )(info, port_shard, port[None, :])
    gate = call(
        gate_kernel,
        arr((length, channels), F32),
        room=24,
        micros=0.1,
        grid=grid,
        in_specs=[hold((rows, width), lambda i: (i, 0)), fixed(w_gate.shape)],
        out_specs=hold((rows, channels), lambda i: (i, 0)),
        after=(chip, slot),
    )(events, w_gate)
    y, past = call(
        within_kernel,
        (arr((length, channels), F32), arr((length, heads), F32)),
        room=24,
        micros=2.0,
        grid=(length // SPAN,),
        in_specs=[
            hold((SPAN, channels), lambda i: (i, 0)),
            hold((SPAN, 2 * nstate), lambda i: (i, 0)),
            hold((heads, SPAN), lambda i: (0, i)),
        ],
        out_specs=(
            hold((SPAN, channels), lambda i: (i, 0)),
            hold((SPAN, heads), lambda i: (i, 0)),
        ),
        scratch_shapes=[pltpu.VMEM((nstate, channels), F32), pltpu.VMEM((8, heads), F32)],
        after=(gate,),
    )(scaled, bc, log_decay)

    carry = call(
        carry_kernel,
        arr((nstate, channels // 2), BF16),
        micros=0.1,
        in_specs=[VMEM] * len(earlier),
        out_specs=VMEM,
        after=(past, slot, far),
    )(*earlier)
    far = tie(far, carry)
    far_x = lax.ppermute(far, "mp", swap)
    far_y = lax.ppermute(far, "groups", swap)
    carry_beside = lax.ppermute(carry, "sub", swap)

    blocks = call(
        norm_kernel,
        (arr((count, width), BF16),) * 4,
        room=24,
        micros=0.1,
        grid=grid,
        in_specs=[
            SMEM,
            hold((rows, channels), lambda i: (i, 0)),
            hold((rows, channels), lambda i: (i, 0)),
            hold((rows, 2 * nstate), lambda i: (i, 0)),
            hold((rows, heads), lambda i: (i, 0)),
            fixed(carry.shape),
            fixed(carry.shape),
            fixed(beside.shape),
            fixed((channels,)),
            fixed(w_out.shape),
            fixed(slot.shape),
        ],
        out_specs=(fixed((count, width)),) * 4,
        scratch_shapes=[pltpu.VMEM((nstate, channels), BF16), pltpu.VMEM((length, width), BF16)],
    )(info, y, gate, bc, past, carry, carry_beside, beside, norm_gain, w_out, slot)
    near = [(i, i ^ 1) for i in range(shard_count)]
    near_x = [(2 * i + j, 2 * (i ^ 1) + (j ^ 1)) for i in range(shard_count) for j in range(2)]
    keep, beside_rows, same, other = blocks
    for piece in (far_x, far_y, own):
        beside_rows, same, other = (tie(a, piece) for a in (beside_rows, same, other))
    terms = (
        keep,
        lax.ppermute(beside_rows, "mp", swap),
        lax.ppermute(same, "tm", near),
        lax.ppermute(other, ("tm", "mp"), near_x),
    )
    own, far, far_y, far_x = (tie(a, keep) for a in (own, far, far_y, far_x))
    far_xy = lax.ppermute(far_x, "groups", swap)
    away, local = call(
        mix_kernel,
        (arr((count, width), BF16),) * 2,
        micros=0.1,
        in_specs=[VMEM] * 5,
        out_specs=(VMEM,) * 2,
    )(*terms, mix_gain)
    own_s, far_s, far_ys, far_xs = (lax.ppermute(a, "sub", swap) for a in (own, far, far_y, far_x))
    far_xys = lax.ppermute(tie(far_xy, away), "sub", swap)

    up, down, shift = call(
        weights_kernel,
        (arr((3, width, width), BF16), arr((3, width, width), BF16), arr((4, width), F32)),
        micros=0.1,
        in_specs=[SMEM, VMEM] + [ANY] * 8,
        out_specs=(VMEM,) * 3,
        scratch_shapes=[pltpu.VMEM((2, TILE, width), BF16), pltpu.SemaphoreType.DMA((16,))],
    )(info, b_up, w_up, w_down, own, own_s, far, far_y, far_s, far_ys)
    same, other, same_l, other_l = call(
        lambda *refs: readout_kernel(cold, *refs),
        (arr((count, side), BF16),) * 4,
        micros=9,
        in_specs=[SMEM, SMEM] + [VMEM] * 5 + [ANY] * 4,
        out_specs=(VMEM,) * 4,
        scratch_shapes=[
            pltpu.VMEM((2, count, width), F32),
            pltpu.VMEM((1, width, width), BF16),
            pltpu.VMEM((1, width, width), BF16),
            pltpu.VMEM((TILE, width), BF16),
            pltpu.SemaphoreType.DMA((9,)),
        ],
    )(info, flag, away, local, shift, up, down, far_x, far_xy, far_xs, far_xys)
    back_same = lax.ppermute(same, "tm", near)
    back_other = lax.ppermute(other, ("tm", "mp"), near_x)
    back_l = lax.ppermute(other_l, "mp", swap)

    return call(
        collect_kernel,
        arr((length, side), BF16),
        micros=1,
        grid=grid,
        in_specs=[hold((rows, 128), lambda i: (i, 0))] + [fixed((count, side))] * 4,
        out_specs=hold((rows, side), lambda i: (i, 0)),
        scratch_shapes=[pltpu.VMEM((4 * count, side), BF16)],
    )(column, same_l, back_l, back_same, back_other)


def shards(*args):
    events, w_inner, w_step = args[0], args[2], args[4]
    sizes = tuple(lax.axis_size(a) for a in ("groups", "tm", "mp", "sub"))
    heads = w_step.shape[1]
    square = events.shape[1] == w_inner.shape[1] == args[12].shape[2]
    if sizes == (2, 4, 2, 2) and heads % 4 == 0 and square and events.shape[0] % 512 == 0:
        return fast(*args)
    return general(*args)


def solution(mesh):
    in_specs = (
        P(("groups", "tm", "sub"), None),
        P(None, "mp"),
        P(None, "mp"),
        P(),
        P(None, "mp"),
        P("mp"),
        P("mp", ("groups", "tm", "sub")),
        P("mp"),
        P("mp", None),
        P(),
        P(("groups", "tm", "sub")),
        P("groups"),
        P("tm", None, "mp"),
        P("tm", "mp"),
        P("tm", "mp", None),
    )
    out_specs = P(("groups", "tm", "sub"), "mp")
    return jax.shard_map(shards, mesh=mesh, in_specs=in_specs, out_specs=out_specs, check_vma=False)
```

```python
import jax
import jax.numpy as jnp
from jax import lax
from jax.experimental import pallas as pl
from jax.experimental.pallas import tpu as pltpu
from jax.sharding import PartitionSpec as P

BLOCK = 256
F32 = jnp.float32
BF16 = jnp.bfloat16


def entering_2(shard, axis, join, neutral):
    place = lax.axis_index(axis)
    gathered = jax.tree.map(
        lambda a, kind: lax.all_gather(a.astype(kind), axis),
        shard,
        jax.tree.map(lambda a: jnp.bfloat16 if a.dtype == jnp.float32 else a.dtype, shard),
    )
    state = jax.tree.map(lambda a, e: jnp.zeros_like(a) + jnp.asarray(e, a.dtype), shard, neutral)

    def one(hop, state):
        return join(
            state,
            jax.tree.map(
                lambda a, own: lax.dynamic_index_in_dim(a, hop, 0, False).astype(own.dtype),
                gathered,
                shard,
            ),
        )

    return lax.fori_loop(0, place, one, state)


def combine_states(earlier, later):
    decay_early, state_early = earlier
    decay_late, state_late = later
    return (decay_early * decay_late, decay_late[:, None, None] * state_early + state_late)


def place_rows(layer_out, mix_gain, placed, shard_count, capacity):
    features = layer_out.shape[1]
    feature_mean = jnp.mean(layer_out * layer_out, axis=1, keepdims=True)
    ready = (layer_out * lax.rsqrt(feature_mean + 1e-05) * mix_gain[None, :]).astype(jnp.bfloat16)
    return (
        jnp.zeros((shard_count * capacity, features), jnp.bfloat16)
        .at[placed]
        .set(ready)
        .reshape(shard_count, capacity, features)
    )


def general(
    events,
    w_gate,
    w_inner,
    w_bc,
    w_step,
    step_bias,
    log_decay,
    norm_gain,
    w_out,
    mix_gain,
    port,
    port_shard,
    w_up,
    b_up,
    w_down,
):
    length = events.shape[0]
    heads_here = w_step.shape[1]
    channels = w_inner.shape[1]
    head_dim = channels // heads_here
    nstate = w_bc.shape[1] // 2
    blocks = length // BLOCK
    gate_pre = jnp.dot(events, w_gate, preferred_element_type=jnp.float32)
    inner_pre = jnp.dot(events, w_inner, preferred_element_type=jnp.float32)
    bc_proj = jnp.dot(events, w_bc, preferred_element_type=jnp.float32).astype(jnp.bfloat16)
    step_size = jax.nn.softplus(
        jnp.dot(events, w_step, preferred_element_type=jnp.float32) + step_bias[None, :]
    )
    scaled = (inner_pre.reshape(length, heads_here, head_dim) * step_size[:, :, None]).astype(
        jnp.bfloat16
    )
    b_blocks = bc_proj[:, :nstate].reshape(blocks, BLOCK, nstate)
    c_blocks = bc_proj[:, nstate:].reshape(blocks, BLOCK, nstate)
    x_blocks = scaled.reshape(blocks, BLOCK, heads_here, head_dim).astype(jnp.float32)
    decay_blocks = log_decay.reshape(heads_here, blocks, BLOCK)
    running = jnp.cumsum(decay_blocks, axis=2)
    causal_mask = jnp.arange(BLOCK)[:, None] >= jnp.arange(BLOCK)[None, :]
    spread = running[:, :, :, None] - running[:, :, None, :]
    weights = jnp.where(causal_mask, jnp.exp(jnp.where(causal_mask, spread, 0.0)), 0.0)
    affinity = jnp.einsum("cin,cjn->cij", c_blocks, b_blocks, preferred_element_type=jnp.float32)
    mixing = affinity[None] * weights
    within = jnp.einsum("hcij,cjhp->cihp", mixing, x_blocks, precision=lax.Precision.HIGHEST)
    to_end = jnp.exp(running[:, :, -1:] - running)
    block_states = jnp.einsum(
        "cjn,hcj,cjhp->chnp",
        b_blocks.astype(jnp.float32),
        to_end,
        x_blocks,
        precision=lax.Precision.HIGHEST,
    )
    block_logs = running[:, :, -1]
    block_decay = jnp.exp(block_logs)
    entering = []
    running_state = jnp.zeros((heads_here, nstate, head_dim), jnp.float32)
    for block_index in range(blocks):
        entering.append(running_state)
        running_state = (
            block_decay[:, block_index][:, None, None] * running_state + block_states[block_index]
        )
    device_decay = jnp.prod(block_decay, axis=1)
    summary = (device_decay, running_state)
    identity = (jnp.ones_like(device_decay), jnp.zeros_like(running_state))
    carried = entering_2(summary, ("tm", "sub"), combine_states, identity)
    carry_state = carried[1]
    before_block = jnp.exp(jnp.cumsum(block_logs, axis=1) - block_logs)
    start_states = jnp.stack(entering) + before_block.T[:, :, None, None] * carry_state[None]
    from_state = jnp.einsum(
        "cin,hci,chnp->cihp",
        c_blocks.astype(jnp.float32),
        jnp.exp(running),
        start_states,
        precision=lax.Precision.HIGHEST,
    )
    ssm_out = (within + from_state).reshape(length, heads_here, head_dim)
    gated = ssm_out * jax.nn.silu(gate_pre.reshape(length, heads_here, head_dim))
    square_mean = jnp.mean(gated * gated, axis=2, keepdims=True)
    normed = (
        (gated * lax.rsqrt(square_mean + 1e-05) * norm_gain.reshape(heads_here, head_dim))
        .reshape(length, channels)
        .astype(jnp.bfloat16)
    )
    partial_sums = jnp.dot(normed, w_out, preferred_element_type=jnp.float32)
    shard_count = lax.axis_size("tm")
    capacity = 2 * length // shard_count
    port_table = port[:, None] == jnp.arange(port_shard.shape[0])[None, :]
    target = jnp.sum(jnp.where(port_table, port_shard[None, :], 0), axis=1)
    target_hot = (target[:, None] == jnp.arange(shard_count)[None, :]).astype(jnp.int32)
    slot_index = jnp.sum((jnp.cumsum(target_hot, axis=0) - 1) * target_hot, axis=1)
    placed = target * capacity + slot_index
    layer_out = lax.psum(partial_sums.astype(jnp.bfloat16), "mp").astype(jnp.float32)
    outgoing = place_rows(layer_out, mix_gain, placed, shard_count, capacity)
    received = lax.all_to_all(outgoing, "tm", split_axis=0, concat_axis=0, tiled=True)
    flat_rows = received.reshape(shard_count * capacity, received.shape[2])
    hidden_units = jax.nn.gelu(
        jnp.dot(flat_rows, w_up[0], preferred_element_type=jnp.float32) + b_up[0][None, :],
        approximate=True,
    ).astype(jnp.bfloat16)
    partial_out = jnp.dot(hidden_units, w_down[0], preferred_element_type=jnp.float32).reshape(
        shard_count, capacity, w_down.shape[2]
    )
    readout = lax.psum_scatter(
        partial_out.astype(jnp.bfloat16), "mp", scatter_dimension=2, tiled=True
    )
    returned = lax.all_to_all(readout, "tm", split_axis=0, concat_axis=0, tiled=True)
    return returned.reshape(shard_count * capacity, returned.shape[2])[placed]


SPAN = 128
TILE = 16
VMEM = pl.BlockSpec(memory_space=pltpu.VMEM)
SMEM = pl.BlockSpec(memory_space=pltpu.SMEM)
ANY = pl.BlockSpec(memory_space=pl.ANY)


def call(kernel, out_shape, *, micros, in_specs, after=(), room=24, **kw):
    count = len(in_specs)

    def body(*refs):
        kernel(*refs[:count], *refs[count + len(after) :])

    run = pl.pallas_call(
        body,
        in_specs=[*in_specs, *[ANY] * len(after)],
        out_shape=out_shape,
        cost_estimate=pl.CostEstimate(
            flops=int(micros * 1e9), bytes_accessed=int(micros * 3e6), transcendentals=0
        ),
        compiler_params=pltpu.CompilerParams(vmem_limit_bytes=room * 1024 * 1024),
        **kw,
    )
    return lambda *args: run(*args, *after)


def arr(shape, kind):
    return jax.ShapeDtypeStruct(shape, kind)


def dot(a, b, left=1, right=0):
    return lax.dot_general(a, b, (((left,), (right,)), ((), ())), preferred_element_type=F32)


def split(v, terms):
    out = []
    for _ in range(terms):
        part = v.astype(BF16)
        out.append(part)
        v = v - part.astype(F32)
    return out


def tie(x, first):
    return lax.optimization_barrier((x, first))[0]


def head_lanes(heads, channels):
    first = iota((heads, channels), 0) * (channels // heads)
    lane = iota((heads, channels), 1)
    return ones_where((lane >= first) & (lane < first + channels // heads))


def spread_heads(v, lanes):
    return dot(jnp.concatenate(split(v, 2), axis=1), jnp.concatenate([lanes, lanes], axis=0))


def iota(shape, dim):
    return lax.broadcasted_iota(jnp.int32, shape, dim)


def ones_where(mask, kind=BF16):
    return jnp.where(mask, 1.0, 0.0).astype(kind)


def scan_in_kernel(ev, w_inner, w_bc, w_step, bias, decay, scaled_o, bc_o, sum_o, state, total):
    step_id = pl.program_id(0)
    rows = ev.shape[0]
    nstate = w_bc.shape[1] // 2
    x = ev[...]
    lanes = head_lanes(decay.shape[0], w_inner.shape[1])
    inner = dot(x, w_inner[...])
    bc = dot(x, w_bc[...]).astype(BF16)
    pre = dot(x, w_step[...], 1, 1) + bias[...]
    step = jnp.maximum(pre, 0.0) + jnp.log1p(jnp.exp(-jnp.abs(pre)))
    scaled = (inner * spread_heads(step, lanes)).astype(BF16)
    scaled_o[...] = scaled
    bc_o[...] = bc
    logs = split(decay[...], 3)
    later = ones_where(iota((rows, rows), 1) > iota((rows, rows), 0))
    to_end = jnp.exp(sum(dot(later, part, 1, 1) for part in logs))
    whole = jnp.exp(sum(dot(jnp.ones((8, rows), BF16), part, 1, 1) for part in logs))
    weighted = (scaled.astype(F32) * spread_heads(to_end, lanes)).astype(BF16)
    fresh = dot(bc[:, :nstate], weighted, 0, 0)
    fade = spread_heads(whole, lanes)

    @pl.when(step_id == 0)
    def _():
        state[...] = fresh
        total[...] = fade

    @pl.when(step_id > 0)
    def _():
        state[...] = state[...] * fade[:1] + fresh
        total[...] = total[...] * fade

    @pl.when(step_id == pl.num_programs(0) - 1)
    def _():
        put_summary(sum_o, state[...], total[:1])


def put_summary(ref, state, decay):
    n, width = state.shape
    ref[:n, :] = state.astype(BF16)
    high = decay.astype(BF16).astype(F32)
    row = iota((TILE, width), 0)
    ref[n:, :] = jnp.where(row == 0, high, jnp.where(row == 1, decay - high, 0.0)).astype(BF16)


def get_summary(value):
    n = value.shape[0] - TILE
    value = value.astype(F32)
    return value[n : n + 1] + value[n + 1 : n + 2], value[:n]


def chip_kernel(info, own, other, out):
    half = out.shape[1]
    place = info[3]
    cols = pl.ds(pl.multiple_of(place * half, half), half)
    mine, theirs = own[:, cols].astype(F32), other[:, cols].astype(F32)
    first = jnp.where(place == 0, mine, theirs)
    second = jnp.where(place == 0, theirs, mine)
    decay_1, state_1 = get_summary(first)
    decay_2, state_2 = get_summary(second)
    put_summary(out, decay_2 * state_1 + state_2, decay_1 * decay_2)


def carry_kernel(*refs):
    out = refs[-1]
    state = None
    for ref in reversed(refs[:-1]):
        decay, fresh = get_summary(ref[...])
        state = fresh if state is None else decay * state + fresh
    out[...] = state.astype(BF16)


def within_kernel(scaled, bc, decay, y_o, past_o, state, run):
    step_id = pl.program_id(0)
    rows = scaled.shape[0]
    heads = decay.shape[0]
    nstate = bc.shape[1] // 2
    pair = scaled.shape[1] * 2 // heads

    @pl.when(step_id == 0)
    def _():
        state[...] = jnp.zeros_like(state)
        run[...] = jnp.zeros_like(run)

    lanes = head_lanes(heads, scaled.shape[1])
    halves = head_lanes(2, pair)
    row, col = iota((rows, rows), 0), iota((rows, rows), 1)
    causal = row >= col
    logs = split(decay[...], 3)
    until = sum(dot(ones_where(causal), part, 1, 1) for part in logs)
    until_row = sum(dot(part, ones_where(row <= col)) for part in logs)
    b, c = bc[:, :nstate], bc[:, nstate:]
    affinity = dot(c, b, 1, 1)
    past = spread_heads(jnp.exp(until), lanes) * dot(c, state[...].astype(BF16))
    for number in range(heads // 2):
        mixes = []
        for head in (2 * number, 2 * number + 1):
            gap = until[:, head : head + 1] - until_row[head : head + 1, :]
            mixes.append((affinity * jnp.exp(jnp.where(causal, gap, -1e30))).astype(BF16))
        cols = slice(number * pair, (number + 1) * pair)
        x = scaled[:, cols]
        both = jnp.concatenate([x * halves[0:1, :], x * halves[1:2, :]], axis=0)
        y_o[:, cols] = past[:, cols] + dot(jnp.concatenate(mixes, axis=1), both)
    last = until[rows - 1 :, :]
    weighted = scaled[...].astype(F32) * spread_heads(jnp.exp(last - until), lanes)
    fade = spread_heads(jnp.exp(jnp.broadcast_to(last, (8, heads))), lanes)
    state[...] = state[...] * fade[:1] + dot(b, weighted.astype(BF16), 0, 0)
    past_o[...] = jnp.exp(until + run[:1])
    run[...] += jnp.broadcast_to(last, run.shape)


def norm_kernel(info, y, gate, bc, past, mine, other, before, gain, w_out, slot, *refs):
    outs, (carry, all_rows) = refs[:4], refs[4:]
    step_id = pl.program_id(0)
    rows, channels = y.shape
    heads = past.shape[1]
    nstate = bc.shape[1] // 2
    lanes = head_lanes(heads, channels)

    @pl.when(step_id == 0)
    def _():
        here = info[3]
        a, b = mine[...].astype(F32), other[...].astype(F32)
        low, high = jnp.where(here == 0, a, b), jnp.where(here == 0, b, a)
        chip = jnp.concatenate([low, high], axis=1)
        decay, state = get_summary(before[...])
        carry[...] = jnp.where(here == 0, chip, decay * chip + state).astype(BF16)

    ssm = y[...] + spread_heads(past[...], lanes) * dot(bc[:, nstate:], carry[...])
    gated = ssm * gate[...]
    square = dot((gated * gated).astype(BF16), lanes, 1, 1) * (heads / channels)
    scale = spread_heads(lax.rsqrt(square + 1e-05), lanes)
    normed = (gated * scale * gain[...][None, :]).astype(BF16)
    all_rows[pl.ds(pl.multiple_of(step_id * rows, rows), rows), :] = dot(normed, w_out[...]).astype(BF16)

    @pl.when(step_id == pl.num_programs(0) - 1)
    def _():
        for number, out in enumerate(outs):
            count = out.shape[0]
            pick = ones_where(slot[...] == iota((count, slot.shape[1]), 0) + number * count)
            out[...] = dot(pick, all_rows[...]).astype(BF16)


def mixed(term_1, term_2, gain):
    total = term_1[...].astype(F32) + term_2[...].astype(F32)
    mean = jnp.mean(total * total, axis=1, keepdims=True)
    return (total * lax.rsqrt(mean + 1e-05) * gain[...][None, :]).astype(BF16)


def mix_kernel(term_1, recv, term_2, keep, gain, away, local):
    away[...] = mixed(term_1, term_2, gain)
    local[...] = mixed(keep, recv, gain)


def route_kernel(cold, info, shard, port, slot_o, column_o, flag_o):
    length = port.shape[1]
    half_rows = 2 * length // 4 // 2
    rows = half_rows + cold
    target = jnp.zeros(port.shape, jnp.int32)
    for number in range(shard.shape[0]):
        target = jnp.where(port[...] == number, shard[number], target)
    group = iota((8, length), 0)
    member = ones_where(jnp.broadcast_to(target, (8, length)) == group, F32)
    lane = iota((8, length), 1)
    count = member
    reach = 1
    while reach < length:
        count = count + jnp.where(lane >= reach, pltpu.roll(count, reach, 1), 0.0)
        reach *= 2
    rank = jnp.sum(member * (count - 1.0), axis=0, keepdims=True).astype(jnp.int32)
    whole = jnp.broadcast_to(count[:, length - 1 :], (8, 128))
    big = jnp.where(whole == 2.0 * half_rows, group[:, :128], 0)
    hot = jnp.max(big.astype(F32)).astype(jnp.int32)
    flag_o[0] = jnp.where(hot == info[0], 0, 1)
    away = target ^ info[0]
    half = (rank & 1) ^ info[1]
    row = rank >> 1
    row = jnp.where(away >= 2, rows - 1 - row, row)
    slot = (2 * (away & 1) + half) * rows + row
    slot_o[...] = slot
    wide = jnp.broadcast_to(slot.astype(F32), (128, length))
    column_o[...] = wide.T.astype(jnp.int32)


def starter(sems):
    copies = []

    def start(source, target):
        copies.append(pltpu.make_async_copy(source, target, sems.at[len(copies)]))
        copies[-1].start()

    return copies, start


def quarters(info, pieces, start, up, down, bank):
    part = up.shape[1] // 4
    for number, piece in enumerate(pieces):
        first = (info[3] ^ (number // 2)) * 2 + (info[2] ^ (number % 2))
        at = pl.ds(pl.multiple_of(first * part, part), part)
        start(piece.at[pl.ds(0, part)], up.at[bank, at])
        start(piece.at[pl.ds(part, part)], down.at[bank, at])


def weights_kernel(info, bias, w_up, w_down, own, own_s, far_1, far_2, far_1s, far_2s, up, down, shift, extra, sems):
    part = up.shape[1] // 4
    copies, start = starter(sems)
    start(w_up.at[0], up.at[0])
    start(w_down.at[0], down.at[0])
    for core, piece in enumerate((own, own_s)):
        at = pl.ds(pl.multiple_of((info[3] ^ core) * 2 * part, 2 * part), 2 * part)
        start(piece.at[pl.ds(0, 2 * part)], up.at[1, at])
        start(piece.at[pl.ds(2 * part, 2 * part)], down.at[1, at])
    quarters(info, (far_1, far_2, far_1s, far_2s), start, up, down, 2)
    start(own.at[pl.ds(4 * part, TILE)], extra.at[0])
    start(far_1.at[pl.ds(2 * part, TILE)], extra.at[1])
    for copy in copies:
        copy.wait()
    rows = [bias[...]] + [jnp.sum(extra[i].astype(F32), axis=0, keepdims=True) for i in range(2)]
    shift[...] = jnp.concatenate(rows + rows[:1], axis=0)


def readout_kernel(cold, info, flag, away, local, shift, up, down, *refs):
    pieces = refs[:4]
    same_o, other_o, same_l_o, other_l_o, total, up_3, down_3, extra, sems = refs[4:]
    copies, start = starter(sems)
    quarters(info, pieces, start, up_3, down_3, 0)
    start(pieces[0].at[pl.ds(up.shape[1] // 2, TILE)], extra)
    count = away.shape[0]

    def run(lo, hi, bank):
        size = hi - lo
        x = jnp.concatenate([away[lo:hi], local[lo:hi]], axis=0)
        out = None
        for half in (0, 1):
            if bank + half == 3:
                for copy in copies:
                    copy.wait()
                v = dot(x, up_3[0]) + jnp.sum(extra[...].astype(F32), axis=0, keepdims=True)
            else:
                v = dot(x, up[bank + half]) + shift[bank + half : bank + half + 1, :]
            hidden = (0.5 * v * (1.0 + jnp.tanh(0.7978845608028654 * (v + 0.044715 * v * v * v)))).astype(BF16)
            y = dot(hidden, down_3[0] if bank + half == 3 else down[bank + half])
            out = y if half == 0 else out + y
        total[0, lo:hi, :] = out[:size]
        total[1, lo:hi, :] = out[size:]

    @pl.when(flag[0] == 0)
    def _():
        run(0, count - cold, 0)
        run(count - cold, count, 2)

    @pl.when(flag[0] != 0)
    def _():
        run(0, cold, 0)
        run(cold, count, 2)

    place = info[1]
    side = same_o.shape[1]
    for number, (near, far) in enumerate(((same_o, other_o), (same_l_o, other_l_o))):
        low, high = total[number, :, :side], total[number, :, side:]
        near[...] = jnp.where(place == 0, low, high).astype(BF16)
        far[...] = jnp.where(place == 0, high, low).astype(BF16)


def payload_kernel(info, bias, w_up, w_down, out, sems):
    part = (out.shape[0] - TILE) // 2
    first = info[3] * (out.shape[1] // 2)
    if 2 * part < out.shape[1] // 2 + part:
        first = first + info[2] * part
    at = pl.ds(pl.multiple_of(first, part), part)
    copies = [
        pltpu.make_async_copy(w.at[0, at], out.at[pl.ds(number * part, part)], sems.at[number])
        for number, w in enumerate((w_up, w_down))
    ]
    for copy in copies:
        copy.start()
    row = iota((TILE, out.shape[1]), 0)
    rows = jnp.zeros((TILE, out.shape[1]), F32)
    for number, term in enumerate(split(bias[...], 3)):
        rows = jnp.where(row == number, term.astype(F32), rows)
    out[2 * part :, :] = rows.astype(BF16)
    for copy in copies:
        copy.wait()


def gate_kernel(ev, w_gate, out):
    gate = dot(ev[...], w_gate[...])
    out[...] = gate / (1.0 + jnp.exp(-gate))


def collect_kernel(column, a, b, c, d, out, joined):
    rows = a.shape[0]

    @pl.when(pl.program_id(0) == 0)
    def _():
        for number, ref in enumerate((a, b, c, d)):
            joined[number * rows : (number + 1) * rows, :] = ref[...]

    place = column[...]
    lane = iota(place.shape, 1)
    picks = [ones_where(place == lane + first) for first in range(0, 4 * rows, 128)]
    out[...] = dot(jnp.concatenate(picks, axis=1), joined[...]).astype(BF16)


def hold(block, index):
    return pl.BlockSpec(block, index)


def fixed(shape):
    return pl.BlockSpec(shape, lambda i: (0,) * len(shape))


def fast(
    events,
    w_gate,
    w_inner,
    w_bc,
    w_step,
    step_bias,
    log_decay,
    norm_gain,
    w_out,
    mix_gain,
    port,
    port_shard,
    w_up,
    b_up,
    w_down,
):
    length, width = events.shape
    channels = w_inner.shape[1]
    heads = w_step.shape[1]
    head_dim = channels // heads
    nstate = w_bc.shape[1] // 2
    shard_count = lax.axis_size("tm")
    hot_rows = 2 * length // shard_count // 2
    most = -(-(length - 2 * hot_rows) // (shard_count - 1))
    cold = -(-((most + 1) // 2) // TILE) * TILE
    count = hot_rows + cold
    info = jnp.stack([lax.axis_index(a) for a in ("tm", "mp", "groups", "sub")]).astype(jnp.int32)
    swap = [(0, 1), (1, 0)]
    side = width // 2

    part = width // 4
    def payload(rows, room, after):
        return call(
            payload_kernel,
            arr((2 * rows + TILE, width), BF16),
            micros=0.001,
            room=room,
            in_specs=[SMEM, VMEM, ANY, ANY],
            out_specs=VMEM,
            scratch_shapes=[pltpu.SemaphoreType.DMA((2,))],
            after=after,
        )(info, b_up, w_up, w_down)

    share = payload(part, 62, ())
    far = lax.ppermute(share, "tm", [(i, i ^ 2) for i in range(shard_count)])

    rows = 2 * SPAN
    grid = (length // rows,)
    scaled, bc, summary = call(
        scan_in_kernel,
        (
            arr((length, channels), BF16),
            arr((length, 2 * nstate), BF16),
            arr((nstate + TILE, channels), BF16),
        ),
        room=62,
        after=(share,),
        micros=0.001,
        grid=grid,
        in_specs=[
            hold((rows, width), lambda i: (i, 0)),
            fixed(w_inner.shape),
            fixed(w_bc.shape),
            fixed((heads, width)),
            fixed((1, heads)),
            hold((heads, rows), lambda i: (0, i)),
        ],
        out_specs=(
            hold((rows, channels), lambda i: (i, 0)),
            hold((rows, 2 * nstate), lambda i: (i, 0)),
            fixed((nstate + TILE, channels)),
        ),
        scratch_shapes=[pltpu.VMEM((nstate, channels), F32), pltpu.VMEM((8, channels), F32)],
    )(events, w_inner, w_bc, w_step.T, step_bias[None, :], log_decay)
    beside = lax.ppermute(summary, "sub", swap)
    chip = call(
        chip_kernel,
        arr((nstate + TILE, channels // 2), BF16),
        micros=0.001,
        in_specs=[SMEM, VMEM, VMEM],
        out_specs=VMEM,
    )(info, summary, beside)
    earlier = [
        lax.ppermute(chip, "tm", [(i, i + hop) for i in range(shard_count - hop)])
        for hop in range(1, shard_count)
    ]

    own = lax.ppermute(payload(2 * part, 24, (summary,)), "mp", swap)
    slot, column, flag = call(
        lambda *refs: route_kernel(cold, *refs),
        (arr((1, length), jnp.int32), arr((length, 128), jnp.int32), arr((1,), jnp.int32)),
        micros=0.001,
        in_specs=[SMEM, SMEM, VMEM],
        out_specs=(VMEM, VMEM, SMEM),
    )(info, port_shard, port[None, :])
    gate = call(
        gate_kernel,
        arr((length, channels), F32),
        room=24,
        micros=0.001,
        grid=grid,
        in_specs=[hold((rows, width), lambda i: (i, 0)), fixed(w_gate.shape)],
        out_specs=hold((rows, channels), lambda i: (i, 0)),
        after=(chip, slot),
    )(events, w_gate)
    y, past = call(
        within_kernel,
        (arr((length, channels), F32), arr((length, heads), F32)),
        room=24,
        micros=0.001,
        grid=(length // SPAN,),
        in_specs=[
            hold((SPAN, channels), lambda i: (i, 0)),
            hold((SPAN, 2 * nstate), lambda i: (i, 0)),
            hold((heads, SPAN), lambda i: (0, i)),
        ],
        out_specs=(
            hold((SPAN, channels), lambda i: (i, 0)),
            hold((SPAN, heads), lambda i: (i, 0)),
        ),
        scratch_shapes=[pltpu.VMEM((nstate, channels), F32), pltpu.VMEM((8, heads), F32)],
        after=(gate,),
    )(scaled, bc, log_decay)

    carry = call(
        carry_kernel,
        arr((nstate, channels // 2), BF16),
        micros=0.001,
        in_specs=[VMEM] * len(earlier),
        out_specs=VMEM,
        after=(past, slot, far),
    )(*earlier)
    far = tie(far, carry)
    far_x = lax.ppermute(far, "mp", swap)
    far_y = lax.ppermute(far, "groups", swap)
    carry_beside = lax.ppermute(carry, "sub", swap)

    wide = 2 * rows
    blocks = call(
        norm_kernel,
        (arr((count, width), BF16),) * 4,
        room=24,
        micros=0.001,
        grid=(length // wide,),
        in_specs=[
            SMEM,
            hold((wide, channels), lambda i: (i, 0)),
            hold((wide, channels), lambda i: (i, 0)),
            hold((wide, 2 * nstate), lambda i: (i, 0)),
            hold((wide, heads), lambda i: (i, 0)),
            fixed(carry.shape),
            fixed(carry.shape),
            fixed(beside.shape),
            fixed((channels,)),
            fixed(w_out.shape),
            fixed(slot.shape),
        ],
        out_specs=(fixed((count, width)),) * 4,
        scratch_shapes=[pltpu.VMEM((nstate, channels), BF16), pltpu.VMEM((length, width), BF16)],
    )(info, y, gate, bc, past, carry, carry_beside, beside, norm_gain, w_out, slot)
    near = [(i, i ^ 1) for i in range(shard_count)]
    near_x = [(2 * i + j, 2 * (i ^ 1) + (j ^ 1)) for i in range(shard_count) for j in range(2)]
    keep, beside_rows, same, other = blocks
    terms = (
        lax.ppermute(same, "tm", near),
        lax.ppermute(beside_rows, "mp", swap),
        lax.ppermute(other, ("tm", "mp"), near_x),
        keep,
    )
    own, far, far_y, far_x = (tie(a, keep) for a in (own, far, far_y, far_x))
    far_xy = lax.ppermute(far_x, "groups", swap)
    away, local = call(
        mix_kernel,
        (arr((count, width), BF16),) * 2,
        micros=5,
        in_specs=[VMEM] * 5,
        out_specs=(VMEM,) * 2,
    )(*terms, mix_gain)
    own_s, far_s, far_ys, far_xs = (lax.ppermute(a, "sub", swap) for a in (own, far, far_y, far_x))
    far_xys = lax.ppermute(tie(far_xy, away), "sub", swap)

    up, down, shift = call(
        weights_kernel,
        (arr((3, width, width), BF16), arr((3, width, width), BF16), arr((4, width), F32)),
        micros=0.1,
        in_specs=[SMEM, VMEM] + [ANY] * 8,
        out_specs=(VMEM,) * 3,
        scratch_shapes=[pltpu.VMEM((2, TILE, width), BF16), pltpu.SemaphoreType.DMA((16,))],
    )(info, b_up, w_up, w_down, own, own_s, far, far_y, far_s, far_ys)
    same, other, same_l, other_l = call(
        lambda *refs: readout_kernel(cold, *refs),
        (arr((count, side), BF16),) * 4,
        micros=9,
        in_specs=[SMEM, SMEM] + [VMEM] * 5 + [ANY] * 4,
        out_specs=(VMEM,) * 4,
        scratch_shapes=[
            pltpu.VMEM((2, count, width), F32),
            pltpu.VMEM((1, width, width), BF16),
            pltpu.VMEM((1, width, width), BF16),
            pltpu.VMEM((TILE, width), BF16),
            pltpu.SemaphoreType.DMA((9,)),
        ],
    )(info, flag, away, local, shift, up, down, far_x, far_xy, far_xs, far_xys)
    back_same = lax.ppermute(same, "tm", near)
    back_other = lax.ppermute(other, ("tm", "mp"), near_x)
    back_l = lax.ppermute(other_l, "mp", swap)

    return call(
        collect_kernel,
        arr((length, side), BF16),
        micros=1,
        grid=(length // (2 * rows),),
        in_specs=[hold((2 * rows, 128), lambda i: (i, 0))] + [fixed((count, side))] * 4,
        out_specs=hold((2 * rows, side), lambda i: (i, 0)),
        scratch_shapes=[pltpu.VMEM((4 * count, side), BF16)],
    )(column, same_l, back_l, back_same, back_other)


def shards(*args):
    events, w_inner, w_step = args[0], args[2], args[4]
    sizes = tuple(lax.axis_size(a) for a in ("groups", "tm", "mp", "sub"))
    heads = w_step.shape[1]
    square = events.shape[1] == w_inner.shape[1] == args[12].shape[2]
    if sizes == (2, 4, 2, 2) and heads % 4 == 0 and square and events.shape[0] % 512 == 0:
        return fast(*args)
    return general(*args)


def solution(mesh):
    in_specs = (
        P(("groups", "tm", "sub"), None),
        P(None, "mp"),
        P(None, "mp"),
        P(),
        P(None, "mp"),
        P("mp"),
        P("mp", ("groups", "tm", "sub")),
        P("mp"),
        P("mp", None),
        P(),
        P(("groups", "tm", "sub")),
        P("groups"),
        P("tm", None, "mp"),
        P("tm", "mp"),
        P("tm", "mp", None),
    )
    out_specs = P(("groups", "tm", "sub"), "mp")
    return jax.shard_map(shards, mesh=mesh, in_specs=in_specs, out_specs=out_specs, check_vma=False)
```

```python
import jax
import jax.numpy as jnp
from jax import lax
from jax.experimental import pallas as pl
from jax.experimental.pallas import tpu as pltpu
from jax.sharding import PartitionSpec as P

BLOCK = 256
F32 = jnp.float32
BF16 = jnp.bfloat16


def entering_2(shard, axis, join, neutral):
    place = lax.axis_index(axis)
    gathered = jax.tree.map(
        lambda a, kind: lax.all_gather(a.astype(kind), axis),
        shard,
        jax.tree.map(lambda a: jnp.bfloat16 if a.dtype == jnp.float32 else a.dtype, shard),
    )
    state = jax.tree.map(lambda a, e: jnp.zeros_like(a) + jnp.asarray(e, a.dtype), shard, neutral)

    def one(hop, state):
        return join(
            state,
            jax.tree.map(
                lambda a, own: lax.dynamic_index_in_dim(a, hop, 0, False).astype(own.dtype),
                gathered,
                shard,
            ),
        )

    return lax.fori_loop(0, place, one, state)


def combine_states(earlier, later):
    decay_early, state_early = earlier
    decay_late, state_late = later
    return (decay_early * decay_late, decay_late[:, None, None] * state_early + state_late)


def place_rows(layer_out, mix_gain, placed, shard_count, capacity):
    features = layer_out.shape[1]
    feature_mean = jnp.mean(layer_out * layer_out, axis=1, keepdims=True)
    ready = (layer_out * lax.rsqrt(feature_mean + 1e-05) * mix_gain[None, :]).astype(jnp.bfloat16)
    return (
        jnp.zeros((shard_count * capacity, features), jnp.bfloat16)
        .at[placed]
        .set(ready)
        .reshape(shard_count, capacity, features)
    )


def general(
    events,
    w_gate,
    w_inner,
    w_bc,
    w_step,
    step_bias,
    log_decay,
    norm_gain,
    w_out,
    mix_gain,
    port,
    port_shard,
    w_up,
    b_up,
    w_down,
):
    length = events.shape[0]
    heads_here = w_step.shape[1]
    channels = w_inner.shape[1]
    head_dim = channels // heads_here
    nstate = w_bc.shape[1] // 2
    blocks = length // BLOCK
    gate_pre = jnp.dot(events, w_gate, preferred_element_type=jnp.float32)
    inner_pre = jnp.dot(events, w_inner, preferred_element_type=jnp.float32)
    bc_proj = jnp.dot(events, w_bc, preferred_element_type=jnp.float32).astype(jnp.bfloat16)
    step_size = jax.nn.softplus(
        jnp.dot(events, w_step, preferred_element_type=jnp.float32) + step_bias[None, :]
    )
    scaled = (inner_pre.reshape(length, heads_here, head_dim) * step_size[:, :, None]).astype(
        jnp.bfloat16
    )
    b_blocks = bc_proj[:, :nstate].reshape(blocks, BLOCK, nstate)
    c_blocks = bc_proj[:, nstate:].reshape(blocks, BLOCK, nstate)
    x_blocks = scaled.reshape(blocks, BLOCK, heads_here, head_dim).astype(jnp.float32)
    decay_blocks = log_decay.reshape(heads_here, blocks, BLOCK)
    running = jnp.cumsum(decay_blocks, axis=2)
    causal_mask = jnp.arange(BLOCK)[:, None] >= jnp.arange(BLOCK)[None, :]
    spread = running[:, :, :, None] - running[:, :, None, :]
    weights = jnp.where(causal_mask, jnp.exp(jnp.where(causal_mask, spread, 0.0)), 0.0)
    affinity = jnp.einsum("cin,cjn->cij", c_blocks, b_blocks, preferred_element_type=jnp.float32)
    mixing = affinity[None] * weights
    within = jnp.einsum("hcij,cjhp->cihp", mixing, x_blocks, precision=lax.Precision.HIGHEST)
    to_end = jnp.exp(running[:, :, -1:] - running)
    block_states = jnp.einsum(
        "cjn,hcj,cjhp->chnp",
        b_blocks.astype(jnp.float32),
        to_end,
        x_blocks,
        precision=lax.Precision.HIGHEST,
    )
    block_logs = running[:, :, -1]
    block_decay = jnp.exp(block_logs)
    entering = []
    running_state = jnp.zeros((heads_here, nstate, head_dim), jnp.float32)
    for block_index in range(blocks):
        entering.append(running_state)
        running_state = (
            block_decay[:, block_index][:, None, None] * running_state + block_states[block_index]
        )
    device_decay = jnp.prod(block_decay, axis=1)
    summary = (device_decay, running_state)
    identity = (jnp.ones_like(device_decay), jnp.zeros_like(running_state))
    carried = entering_2(summary, ("tm", "sub"), combine_states, identity)
    carry_state = carried[1]
    before_block = jnp.exp(jnp.cumsum(block_logs, axis=1) - block_logs)
    start_states = jnp.stack(entering) + before_block.T[:, :, None, None] * carry_state[None]
    from_state = jnp.einsum(
        "cin,hci,chnp->cihp",
        c_blocks.astype(jnp.float32),
        jnp.exp(running),
        start_states,
        precision=lax.Precision.HIGHEST,
    )
    ssm_out = (within + from_state).reshape(length, heads_here, head_dim)
    gated = ssm_out * jax.nn.silu(gate_pre.reshape(length, heads_here, head_dim))
    square_mean = jnp.mean(gated * gated, axis=2, keepdims=True)
    normed = (
        (gated * lax.rsqrt(square_mean + 1e-05) * norm_gain.reshape(heads_here, head_dim))
        .reshape(length, channels)
        .astype(jnp.bfloat16)
    )
    partial_sums = jnp.dot(normed, w_out, preferred_element_type=jnp.float32)
    shard_count = lax.axis_size("tm")
    capacity = 2 * length // shard_count
    port_table = port[:, None] == jnp.arange(port_shard.shape[0])[None, :]
    target = jnp.sum(jnp.where(port_table, port_shard[None, :], 0), axis=1)
    target_hot = (target[:, None] == jnp.arange(shard_count)[None, :]).astype(jnp.int32)
    slot_index = jnp.sum((jnp.cumsum(target_hot, axis=0) - 1) * target_hot, axis=1)
    placed = target * capacity + slot_index
    layer_out = lax.psum(partial_sums.astype(jnp.bfloat16), "mp").astype(jnp.float32)
    outgoing = place_rows(layer_out, mix_gain, placed, shard_count, capacity)
    received = lax.all_to_all(outgoing, "tm", split_axis=0, concat_axis=0, tiled=True)
    flat_rows = received.reshape(shard_count * capacity, received.shape[2])
    hidden_units = jax.nn.gelu(
        jnp.dot(flat_rows, w_up[0], preferred_element_type=jnp.float32) + b_up[0][None, :],
        approximate=True,
    ).astype(jnp.bfloat16)
    partial_out = jnp.dot(hidden_units, w_down[0], preferred_element_type=jnp.float32).reshape(
        shard_count, capacity, w_down.shape[2]
    )
    readout = lax.psum_scatter(
        partial_out.astype(jnp.bfloat16), "mp", scatter_dimension=2, tiled=True
    )
    returned = lax.all_to_all(readout, "tm", split_axis=0, concat_axis=0, tiled=True)
    return returned.reshape(shard_count * capacity, returned.shape[2])[placed]


SPAN = 128
TILE = 16
VMEM = pl.BlockSpec(memory_space=pltpu.VMEM)
SMEM = pl.BlockSpec(memory_space=pltpu.SMEM)
ANY = pl.BlockSpec(memory_space=pl.ANY)


def call(kernel, out_shape, *, micros, in_specs, after=(), room=24, **kw):
    count = len(in_specs)

    def body(*refs):
        kernel(*refs[:count], *refs[count + len(after) :])

    run = pl.pallas_call(
        body,
        in_specs=[*in_specs, *[ANY] * len(after)],
        out_shape=out_shape,
        cost_estimate=pl.CostEstimate(
            flops=int(micros * 1e9), bytes_accessed=int(micros * 3e6), transcendentals=0
        ),
        compiler_params=pltpu.CompilerParams(vmem_limit_bytes=room * 1024 * 1024),
        **kw,
    )
    return lambda *args: run(*args, *after)


def arr(shape, kind):
    return jax.ShapeDtypeStruct(shape, kind)


def dot(a, b, left=1, right=0):
    return lax.dot_general(a, b, (((left,), (right,)), ((), ())), preferred_element_type=F32)


def split(v, terms):
    out = []
    for _ in range(terms):
        part = v.astype(BF16)
        out.append(part)
        v = v - part.astype(F32)
    return out


def tie(x, first):
    return lax.optimization_barrier((x, first))[0]


def head_lanes(heads, channels):
    first = iota((heads, channels), 0) * (channels // heads)
    lane = iota((heads, channels), 1)
    return ones_where((lane >= first) & (lane < first + channels // heads))


def spread_heads(v, lanes):
    return dot(jnp.concatenate(split(v, 2), axis=1), jnp.concatenate([lanes, lanes], axis=0))


def iota(shape, dim):
    return lax.broadcasted_iota(jnp.int32, shape, dim)


def ones_where(mask, kind=BF16):
    return jnp.where(mask, 1.0, 0.0).astype(kind)


def scan_in_kernel(ev, w_inner, w_bc, w_step, bias, decay, scaled_o, bc_o, sum_o, state, total):
    step_id = pl.program_id(0)
    rows = ev.shape[0]
    nstate = w_bc.shape[1] // 2
    x = ev[...]
    lanes = head_lanes(decay.shape[0], w_inner.shape[1])
    inner = dot(x, w_inner[...])
    bc = dot(x, w_bc[...]).astype(BF16)
    pre = dot(x, w_step[...], 1, 1) + bias[...]
    step = jnp.maximum(pre, 0.0) + jnp.log1p(jnp.exp(-jnp.abs(pre)))
    scaled = (inner * spread_heads(step, lanes)).astype(BF16)
    scaled_o[...] = scaled
    bc_o[...] = bc
    logs = split(decay[...], 3)
    later = ones_where(iota((rows, rows), 1) > iota((rows, rows), 0))
    to_end = jnp.exp(sum(dot(later, part, 1, 1) for part in logs))
    whole = jnp.exp(sum(dot(jnp.ones((8, rows), BF16), part, 1, 1) for part in logs))
    weighted = (scaled.astype(F32) * spread_heads(to_end, lanes)).astype(BF16)
    fresh = dot(bc[:, :nstate], weighted, 0, 0)
    fade = spread_heads(whole, lanes)

    @pl.when(step_id == 0)
    def _():
        state[...] = fresh
        total[...] = fade

    @pl.when(step_id > 0)
    def _():
        state[...] = state[...] * fade[:1] + fresh
        total[...] = total[...] * fade

    @pl.when(step_id == pl.num_programs(0) - 1)
    def _():
        put_summary(sum_o, state[...], total[:1])


def put_summary(ref, state, decay):
    n, width = state.shape
    ref[:n, :] = state.astype(BF16)
    high = decay.astype(BF16).astype(F32)
    row = iota((TILE, width), 0)
    ref[n:, :] = jnp.where(row == 0, high, jnp.where(row == 1, decay - high, 0.0)).astype(BF16)


def get_summary(value):
    n = value.shape[0] - TILE
    value = value.astype(F32)
    return value[n : n + 1] + value[n + 1 : n + 2], value[:n]


def chip_kernel(info, own, other, out):
    half = out.shape[1]
    place = info[3]
    cols = pl.ds(pl.multiple_of(place * half, half), half)
    mine, theirs = own[:, cols].astype(F32), other[:, cols].astype(F32)
    first = jnp.where(place == 0, mine, theirs)
    second = jnp.where(place == 0, theirs, mine)
    decay_1, state_1 = get_summary(first)
    decay_2, state_2 = get_summary(second)
    put_summary(out, decay_2 * state_1 + state_2, decay_1 * decay_2)


def carry_kernel(*refs):
    out = refs[-1]
    state = None
    for ref in reversed(refs[:-1]):
        decay, fresh = get_summary(ref[...])
        state = fresh if state is None else decay * state + fresh
    out[...] = state.astype(BF16)


def within_kernel(scaled, bc, decay, y_o, past_o, state, run):
    step_id = pl.program_id(0)
    rows = scaled.shape[0]
    heads = decay.shape[0]
    nstate = bc.shape[1] // 2
    pair = scaled.shape[1] * 2 // heads

    @pl.when(step_id == 0)
    def _():
        state[...] = jnp.zeros_like(state)
        run[...] = jnp.zeros_like(run)

    lanes = head_lanes(heads, scaled.shape[1])
    halves = head_lanes(2, pair)
    row, col = iota((rows, rows), 0), iota((rows, rows), 1)
    causal = row >= col
    logs = split(decay[...], 3)
    until = sum(dot(ones_where(causal), part, 1, 1) for part in logs)
    until_row = sum(dot(part, ones_where(row <= col)) for part in logs)
    b, c = bc[:, :nstate], bc[:, nstate:]
    affinity = dot(c, b, 1, 1)
    past = spread_heads(jnp.exp(until), lanes) * dot(c, state[...].astype(BF16))
    for number in range(heads // 2):
        mixes = []
        for head in (2 * number, 2 * number + 1):
            gap = until[:, head : head + 1] - until_row[head : head + 1, :]
            mixes.append((affinity * jnp.exp(jnp.where(causal, gap, -1e30))).astype(BF16))
        cols = slice(number * pair, (number + 1) * pair)
        x = scaled[:, cols]
        both = jnp.concatenate([x * halves[0:1, :], x * halves[1:2, :]], axis=0)
        y_o[:, cols] = past[:, cols] + dot(jnp.concatenate(mixes, axis=1), both)
    last = until[rows - 1 :, :]
    weighted = scaled[...].astype(F32) * spread_heads(jnp.exp(last - until), lanes)
    fade = spread_heads(jnp.exp(jnp.broadcast_to(last, (8, heads))), lanes)
    state[...] = state[...] * fade[:1] + dot(b, weighted.astype(BF16), 0, 0)
    past_o[...] = jnp.exp(until + run[:1])
    run[...] += jnp.broadcast_to(last, run.shape)


def norm_kernel(info, y, gate, bc, past, mine, other, before, gain, w_out, slot, *refs):
    outs, (carry, all_rows) = refs[:4], refs[4:]
    step_id = pl.program_id(0)
    rows, channels = y.shape
    heads = past.shape[1]
    nstate = bc.shape[1] // 2
    lanes = head_lanes(heads, channels)

    @pl.when(step_id == 0)
    def _():
        here = info[3]
        a, b = mine[...].astype(F32), other[...].astype(F32)
        low, high = jnp.where(here == 0, a, b), jnp.where(here == 0, b, a)
        chip = jnp.concatenate([low, high], axis=1)
        decay, state = get_summary(before[...])
        carry[...] = jnp.where(here == 0, chip, decay * chip + state).astype(BF16)

    ssm = y[...] + spread_heads(past[...], lanes) * dot(bc[:, nstate:], carry[...])
    gated = ssm * gate[...]
    square = dot((gated * gated).astype(BF16), lanes, 1, 1) * (heads / channels)
    scale = spread_heads(lax.rsqrt(square + 1e-05), lanes)
    normed = (gated * scale * gain[...][None, :]).astype(BF16)
    all_rows[pl.ds(pl.multiple_of(step_id * rows, rows), rows), :] = dot(normed, w_out[...]).astype(BF16)

    @pl.when(step_id == pl.num_programs(0) - 1)
    def _():
        for number, out in enumerate(outs):
            count = out.shape[0]
            pick = ones_where(slot[...] == iota((count, slot.shape[1]), 0) + number * count)
            out[...] = dot(pick, all_rows[...]).astype(BF16)


def mixed(term_1, term_2, gain):
    total = term_1[...].astype(F32) + term_2[...].astype(F32)
    mean = jnp.mean(total * total, axis=1, keepdims=True)
    return (total * lax.rsqrt(mean + 1e-05) * gain[...][None, :]).astype(BF16)


def mix_kernel(term_1, recv, term_2, keep, gain, away, local):
    away[...] = mixed(term_1, term_2, gain)
    local[...] = mixed(keep, recv, gain)


def route_kernel(cold, info, shard, port, slot_o, column_o, flag_o):
    length = port.shape[1]
    half_rows = 2 * length // 4 // 2
    rows = half_rows + cold
    target = jnp.zeros(port.shape, jnp.int32)
    for number in range(shard.shape[0]):
        target = jnp.where(port[...] == number, shard[number], target)
    group = iota((8, length), 0)
    member = ones_where(jnp.broadcast_to(target, (8, length)) == group, F32)
    lane = iota((8, length), 1)
    count = member
    reach = 1
    while reach < length:
        count = count + jnp.where(lane >= reach, pltpu.roll(count, reach, 1), 0.0)
        reach *= 2
    rank = jnp.sum(member * (count - 1.0), axis=0, keepdims=True).astype(jnp.int32)
    whole = jnp.broadcast_to(count[:, length - 1 :], (8, 128))
    big = jnp.where(whole == 2.0 * half_rows, group[:, :128], 0)
    hot = jnp.max(big.astype(F32)).astype(jnp.int32)
    flag_o[0] = jnp.where(hot == info[0], 0, 1)
    away = target ^ info[0]
    half = (rank & 1) ^ info[1]
    row = rank >> 1
    row = jnp.where(away >= 2, rows - 1 - row, row)
    slot = (2 * (away & 1) + half) * rows + row
    slot_o[...] = slot
    wide = jnp.broadcast_to(slot.astype(F32), (128, length))
    column_o[...] = wide.T.astype(jnp.int32)


def starter(sems):
    copies = []

    def start(source, target):
        copies.append(pltpu.make_async_copy(source, target, sems.at[len(copies)]))
        copies[-1].start()

    return copies, start


def quarters(info, pieces, start, up, down, bank):
    part = up.shape[1] // 4
    for number, piece in enumerate(pieces):
        first = (info[3] ^ (number // 2)) * 2 + (info[2] ^ (number % 2))
        at = pl.ds(pl.multiple_of(first * part, part), part)
        start(piece.at[pl.ds(0, part)], up.at[bank, at])
        start(piece.at[pl.ds(part, part)], down.at[bank, at])


def weights_kernel(info, bias, w_up, w_down, own, own_s, far_1, far_2, far_1s, far_2s, up, down, shift, extra, sems):
    part = up.shape[1] // 4
    copies, start = starter(sems)
    start(w_up.at[0], up.at[0])
    start(w_down.at[0], down.at[0])
    for core, piece in enumerate((own, own_s)):
        at = pl.ds(pl.multiple_of((info[3] ^ core) * 2 * part, 2 * part), 2 * part)
        start(piece.at[pl.ds(0, 2 * part)], up.at[1, at])
        start(piece.at[pl.ds(2 * part, 2 * part)], down.at[1, at])
    quarters(info, (far_1, far_2, far_1s, far_2s), start, up, down, 2)
    start(own.at[pl.ds(4 * part, TILE)], extra.at[0])
    start(far_1.at[pl.ds(2 * part, TILE)], extra.at[1])
    for copy in copies:
        copy.wait()
    rows = [bias[...]] + [jnp.sum(extra[i].astype(F32), axis=0, keepdims=True) for i in range(2)]
    shift[...] = jnp.concatenate(rows + rows[:1], axis=0)


def readout_kernel(cold, info, flag, away, local, shift, up, down, *refs):
    pieces = refs[:4]
    same_o, other_o, same_l_o, other_l_o, total, up_3, down_3, extra, sems = refs[4:]
    copies, start = starter(sems)
    quarters(info, pieces, start, up_3, down_3, 0)
    start(pieces[0].at[pl.ds(up.shape[1] // 2, TILE)], extra)
    count = away.shape[0]

    def run(lo, hi, bank):
        size = hi - lo
        x = jnp.concatenate([away[lo:hi], local[lo:hi]], axis=0)
        out = None
        for half in (0, 1):
            if bank + half == 3:
                for copy in copies:
                    copy.wait()
                v = dot(x, up_3[0]) + jnp.sum(extra[...].astype(F32), axis=0, keepdims=True)
            else:
                v = dot(x, up[bank + half]) + shift[bank + half : bank + half + 1, :]
            hidden = (0.5 * v * (1.0 + jnp.tanh(0.7978845608028654 * (v + 0.044715 * v * v * v)))).astype(BF16)
            y = dot(hidden, down_3[0] if bank + half == 3 else down[bank + half])
            out = y if half == 0 else out + y
        total[0, lo:hi, :] = out[:size]
        total[1, lo:hi, :] = out[size:]

    @pl.when(flag[0] == 0)
    def _():
        run(0, count - cold, 0)
        run(count - cold, count, 2)

    @pl.when(flag[0] != 0)
    def _():
        run(0, cold, 0)
        run(cold, count, 2)

    place = info[1]
    side = same_o.shape[1]
    for number, (near, far) in enumerate(((same_o, other_o), (same_l_o, other_l_o))):
        low, high = total[number, :, :side], total[number, :, side:]
        near[...] = jnp.where(place == 0, low, high).astype(BF16)
        far[...] = jnp.where(place == 0, high, low).astype(BF16)


def payload_kernel(bias, w_up, w_down, own, share, sems):
    copies = []
    for out, shift in ((share, lax.axis_index("groups")), (own, 0)):
        part = (out.shape[0] - TILE) // 2
        first = lax.axis_index("sub") * (out.shape[1] // 2) + shift * part
        at = pl.ds(pl.multiple_of(first, part), part)
        for number, w in enumerate((w_up, w_down)):
            target = out.at[pl.ds(number * part, part)]
            copies.append(pltpu.make_async_copy(w.at[0, at], target, sems.at[len(copies)]))
            copies[-1].start()
    row = iota((TILE, own.shape[1]), 0)
    rows = jnp.zeros((TILE, own.shape[1]), F32)
    for number, term in enumerate(split(bias[...], 3)):
        rows = jnp.where(row == number, term.astype(F32), rows)
    for out in (own, share):
        out[out.shape[0] - TILE :, :] = rows.astype(BF16)
    for copy in copies:
        copy.wait()


def gate_kernel(ev, w_gate, out):
    gate = dot(ev[...], w_gate[...])
    out[...] = gate / (1.0 + jnp.exp(-gate))


def collect_kernel(column, a, b, c, d, out, joined):
    rows = a.shape[0]

    @pl.when(pl.program_id(0) == 0)
    def _():
        for number, ref in enumerate((a, b, c, d)):
            joined[number * rows : (number + 1) * rows, :] = ref[...]

    place = column[...]
    lane = iota(place.shape, 1)
    picks = [ones_where(place == lane + first) for first in range(0, 4 * rows, 128)]
    out[...] = dot(jnp.concatenate(picks, axis=1), joined[...]).astype(BF16)


def hold(block, index):
    return pl.BlockSpec(block, index)


def fixed(shape):
    return pl.BlockSpec(shape, lambda i: (0,) * len(shape))


def fast(
    events,
    w_gate,
    w_inner,
    w_bc,
    w_step,
    step_bias,
    log_decay,
    norm_gain,
    w_out,
    mix_gain,
    port,
    port_shard,
    w_up,
    b_up,
    w_down,
):
    length, width = events.shape
    channels = w_inner.shape[1]
    heads = w_step.shape[1]
    head_dim = channels // heads
    nstate = w_bc.shape[1] // 2
    shard_count = lax.axis_size("tm")
    hot_rows = 2 * length // shard_count // 2
    most = -(-(length - 2 * hot_rows) // (shard_count - 1))
    cold = -(-((most + 1) // 2) // TILE) * TILE
    count = hot_rows + cold
    info = jnp.stack([lax.axis_index(a) for a in ("tm", "mp", "groups", "sub")]).astype(jnp.int32)
    swap = [(0, 1), (1, 0)]
    side = width // 2

    part = width // 4
    half, share = call(
        payload_kernel,
        (arr((4 * part + TILE, width), BF16), arr((2 * part + TILE, width), BF16)),
        micros=0.001,
        room=62,
        in_specs=[VMEM, ANY, ANY],
        out_specs=(VMEM, VMEM),
        scratch_shapes=[pltpu.SemaphoreType.DMA((4,))],
    )(b_up, w_up, w_down)
    far = lax.ppermute(share, "tm", [(i, i ^ 2) for i in range(shard_count)])

    rows = 2 * SPAN
    grid = (length // rows,)
    scaled, bc, summary = call(
        scan_in_kernel,
        (
            arr((length, channels), BF16),
            arr((length, 2 * nstate), BF16),
            arr((nstate + TILE, channels), BF16),
        ),
        room=62,
        after=(share,),
        micros=0.001,
        grid=grid,
        in_specs=[
            hold((rows, width), lambda i: (i, 0)),
            fixed(w_inner.shape),
            fixed(w_bc.shape),
            fixed((heads, width)),
            fixed((1, heads)),
            hold((heads, rows), lambda i: (0, i)),
        ],
        out_specs=(
            hold((rows, channels), lambda i: (i, 0)),
            hold((rows, 2 * nstate), lambda i: (i, 0)),
            fixed((nstate + TILE, channels)),
        ),
        scratch_shapes=[pltpu.VMEM((nstate, channels), F32), pltpu.VMEM((8, channels), F32)],
    )(events, w_inner, w_bc, w_step.T, step_bias[None, :], log_decay)
    beside = lax.ppermute(summary, "sub", swap)
    chip = call(
        chip_kernel,
        arr((nstate + TILE, channels // 2), BF16),
        micros=0.001,
        in_specs=[SMEM, VMEM, VMEM],
        out_specs=VMEM,
    )(info, summary, beside)
    earlier = [
        lax.ppermute(chip, "tm", [(i, i + hop) for i in range(shard_count - hop)])
        for hop in range(1, shard_count)
    ]

    own = lax.ppermute(tie(half, summary), "mp", swap)
    slot, column, flag = call(
        lambda *refs: route_kernel(cold, *refs),
        (arr((1, length), jnp.int32), arr((length, 128), jnp.int32), arr((1,), jnp.int32)),
        micros=0.001,
        in_specs=[SMEM, SMEM, VMEM],
        out_specs=(VMEM, VMEM, SMEM),
    )(info, port_shard, port[None, :])
    gate = call(
        gate_kernel,
        arr((length, channels), F32),
        room=24,
        micros=0.001,
        grid=grid,
        in_specs=[hold((rows, width), lambda i: (i, 0)), fixed(w_gate.shape)],
        out_specs=hold((rows, channels), lambda i: (i, 0)),
        after=(chip, slot),
    )(events, w_gate)
    y, past = call(
        within_kernel,
        (arr((length, channels), F32), arr((length, heads), F32)),
        room=24,
        micros=0.001,
        grid=(length // SPAN,),
        in_specs=[
            hold((SPAN, channels), lambda i: (i, 0)),
            hold((SPAN, 2 * nstate), lambda i: (i, 0)),
            hold((heads, SPAN), lambda i: (0, i)),
        ],
        out_specs=(
            hold((SPAN, channels), lambda i: (i, 0)),
            hold((SPAN, heads), lambda i: (i, 0)),
        ),
        scratch_shapes=[pltpu.VMEM((nstate, channels), F32), pltpu.VMEM((8, heads), F32)],
        after=(gate,),
    )(scaled, bc, log_decay)

    carry = call(
        carry_kernel,
        arr((nstate, channels // 2), BF16),
        micros=0.001,
        in_specs=[VMEM] * len(earlier),
        out_specs=VMEM,
        after=(past, slot, far),
    )(*earlier)
    far = tie(far, carry)
    far_x = lax.ppermute(far, "mp", swap)
    far_y = lax.ppermute(far, "groups", swap)
    carry_beside = lax.ppermute(carry, "sub", swap)

    wide = 2 * rows
    blocks = call(
        norm_kernel,
        (arr((count, width), BF16),) * 4,
        room=24,
        micros=0.001,
        grid=(length // wide,),
        in_specs=[
            SMEM,
            hold((wide, channels), lambda i: (i, 0)),
            hold((wide, channels), lambda i: (i, 0)),
            hold((wide, 2 * nstate), lambda i: (i, 0)),
            hold((wide, heads), lambda i: (i, 0)),
            fixed(carry.shape),
            fixed(carry.shape),
            fixed(beside.shape),
            fixed((channels,)),
            fixed(w_out.shape),
            fixed(slot.shape),
        ],
        out_specs=(fixed((count, width)),) * 4,
        scratch_shapes=[pltpu.VMEM((nstate, channels), BF16), pltpu.VMEM((length, width), BF16)],
    )(info, y, gate, bc, past, carry, carry_beside, beside, norm_gain, w_out, slot)
    near = [(i, i ^ 1) for i in range(shard_count)]
    near_x = [(2 * i + j, 2 * (i ^ 1) + (j ^ 1)) for i in range(shard_count) for j in range(2)]
    keep, beside_rows, same, other = blocks
    terms = (
        lax.ppermute(same, "tm", near),
        lax.ppermute(beside_rows, "mp", swap),
        lax.ppermute(other, ("tm", "mp"), near_x),
        keep,
    )
    own, far, far_y, far_x = (tie(a, keep) for a in (own, far, far_y, far_x))
    far_xy = lax.ppermute(far_x, "groups", swap)
    away, local = call(
        mix_kernel,
        (arr((count, width), BF16),) * 2,
        micros=5,
        in_specs=[VMEM] * 5,
        out_specs=(VMEM,) * 2,
    )(*terms, mix_gain)
    own_s, far_s, far_ys, far_xs = (lax.ppermute(a, "sub", swap) for a in (own, far, far_y, far_x))
    far_xys = lax.ppermute(tie(far_xy, away), "sub", swap)

    up, down, shift = call(
        weights_kernel,
        (arr((3, width, width), BF16), arr((3, width, width), BF16), arr((4, width), F32)),
        micros=0.1,
        in_specs=[SMEM, VMEM] + [ANY] * 8,
        out_specs=(VMEM,) * 3,
        scratch_shapes=[pltpu.VMEM((2, TILE, width), BF16), pltpu.SemaphoreType.DMA((16,))],
    )(info, b_up, w_up, w_down, own, own_s, far, far_y, far_s, far_ys)
    same, other, same_l, other_l = call(
        lambda *refs: readout_kernel(cold, *refs),
        (arr((count, side), BF16),) * 4,
        micros=9,
        in_specs=[SMEM, SMEM] + [VMEM] * 5 + [ANY] * 4,
        out_specs=(VMEM,) * 4,
        scratch_shapes=[
            pltpu.VMEM((2, count, width), F32),
            pltpu.VMEM((1, width, width), BF16),
            pltpu.VMEM((1, width, width), BF16),
            pltpu.VMEM((TILE, width), BF16),
            pltpu.SemaphoreType.DMA((9,)),
        ],
    )(info, flag, away, local, shift, up, down, far_x, far_xy, far_xs, far_xys)
    back_same = lax.ppermute(same, "tm", near)
    back_other = lax.ppermute(other, ("tm", "mp"), near_x)
    back_l = lax.ppermute(other_l, "mp", swap)

    return call(
        collect_kernel,
        arr((length, side), BF16),
        micros=1,
        grid=(length // (2 * rows),),
        in_specs=[hold((2 * rows, 128), lambda i: (i, 0))] + [fixed((count, side))] * 4,
        out_specs=hold((2 * rows, side), lambda i: (i, 0)),
        scratch_shapes=[pltpu.VMEM((4 * count, side), BF16)],
    )(column, same_l, back_l, back_same, back_other)


def shards(*args):
    events, w_inner, w_step = args[0], args[2], args[4]
    sizes = tuple(lax.axis_size(a) for a in ("groups", "tm", "mp", "sub"))
    heads = w_step.shape[1]
    square = events.shape[1] == w_inner.shape[1] == args[12].shape[2]
    if sizes == (2, 4, 2, 2) and heads % 4 == 0 and square and events.shape[0] % 512 == 0:
        return fast(*args)
    return general(*args)


def solution(mesh):
    in_specs = (
        P(("groups", "tm", "sub"), None),
        P(None, "mp"),
        P(None, "mp"),
        P(),
        P(None, "mp"),
        P("mp"),
        P("mp", ("groups", "tm", "sub")),
        P("mp"),
        P("mp", None),
        P(),
        P(("groups", "tm", "sub")),
        P("groups"),
        P("tm", None, "mp"),
        P("tm", "mp"),
        P("tm", "mp", None),
    )
    out_specs = P(("groups", "tm", "sub"), "mp")
    return jax.shard_map(shards, mesh=mesh, in_specs=in_specs, out_specs=out_specs, check_vma=False)
```
